256 devices in a mesh: row: 32 (over x_lo, z, core), rep: 8 (over x_hi, y).
Axes of the slice: x: 4 (x_hi: 2, x_lo: 2; x = x_hi * 2 + x_lo), y: 4, z: 8, core: 2. Of those that a mesh axis runs over, the one named last changes fastest.
Arguments:
- node_features: bfloat16 [32768, 768], P(('row', 'rep')), may hold values from -6 to 6
- self_weight: bfloat16 [768, 256], replicated, may hold values from -0.21875 to 0.21875
- neigh_weight: bfloat16 [768, 256], replicated, may hold values from -0.21875 to 0.21875
- bias: float32 [256], replicated, may hold values from -4 to 4
- block_values: bfloat16 [32, 32, 8, 128, 128], P('row', 'rep'), as said below
- block_coords: int32 [32, 32, 8, 2], P('row', 'rep'), may hold values from 0 to 7, as said below
- block_counts: int32 [32, 32], P('row', 'rep'), may hold values from 0 to 8, as said below
- out_grad: bfloat16 [32768, 256], P(('row', 'rep')), may hold values from -6 to 6
Outputs:
- activations: bfloat16 [32768, 256], P(('row', 'rep'))
- feature_grad: bfloat16 [32768, 768], P(('row', 'rep'))
- self_grad: float32 [768, 256], replicated
- neigh_grad: float32 [768, 256], replicated
- bias_grad: float32 [256], replicated
The draws below stay inside these ranges and needn't reach their ends.
Inputs may be any that keep to these rules, and one draw needn't show every extreme that they name: block_counts[i, j] equals block_counts[j, i]; every diagonal tile pair has all 8 slots live. `block_coords`: slot b of tile pair (j, i) has the coordinates of slot b of (i, j) swapped; for a diagonal tile pair, slot 7 - b has the coordinates of slot b swapped. `block_values`: slot b of tile pair (j, i) holds the transpose of slot b of (i, j); for a diagonal tile pair, slot 7 - b holds the transpose of slot b; so A is symmetric.
All inputs are finite; a program needn't handle non-finite values.
Results may differ from the reference program's by a relative error of at most 0.017.
Values may be sent and summed in bfloat16 or wider, within the bound.
A program may use at most 64 MiB of HBM per device.

```python
import jax
import jax.numpy as jnp
from jax import lax

FIN = 768
FO = 256
BLK = 128
BR = 8
MAXB = 8
SLABS = 32
NODES = 32768


def pair_masks(extra):
    first = jnp.arange(SLABS).reshape((SLABS, 1, 1) + (1,) * extra)
    second = jnp.arange(SLABS).reshape((1, SLABS, 1) + (1,) * extra)
    slot = jnp.arange(MAXB).reshape((1, 1, MAXB) + (1,) * extra)
    return (first < second, first > second, slot < MAXB // 2)


def draw_block_values(key, part):
    key = jax.random.fold_in(key, 3)
    shape = (SLABS, SLABS, MAXB, BLK, BLK)
    spread = (BLK * MAXB * (1 + SLABS // 5) / BR) ** (-0.5)
    raw = jax.random.normal(key, shape, jnp.float32) * spread
    upper, lower, early = pair_masks(2)
    across = jnp.swapaxes(jnp.swapaxes(raw, 0, 1), 3, 4)
    within = jnp.swapaxes(raw[:, :, ::-1], 3, 4)
    mirrored = jnp.where(upper, raw, jnp.where(lower, across, jnp.where(early, raw, within)))
    return mirrored.astype(jnp.bfloat16)


def draw_block_coords(key, part):
    key = jax.random.fold_in(key, 5)
    raw = jax.random.randint(key, (SLABS, SLABS, MAXB, 2), 0, BR, dtype=jnp.int32)
    swapped = raw[..., ::-1]
    upper, lower, early = pair_masks(1)
    across = jnp.swapaxes(swapped, 0, 1)
    within = swapped[:, :, ::-1]
    return jnp.where(upper, raw, jnp.where(lower, across, jnp.where(early, raw, within))).astype(jnp.int32)


def draw_block_counts(key, part):
    key = jax.random.fold_in(key, 7)
    hub_key, base_key = jax.random.split(key)
    hubness = jax.random.randint(hub_key, (SLABS,), 1, 5, dtype=jnp.int32)
    base = jax.random.randint(base_key, (SLABS, SLABS), 0, MAXB // 2 + 1, dtype=jnp.int32)
    first = jnp.arange(SLABS)[:, None]
    second = jnp.arange(SLABS)[None, :]
    base = jnp.where(first <= second, base, base.T)
    counts = jnp.minimum(MAXB, base * hubness[:, None] * hubness[None, :] // 8)
    return jnp.where(first == second, MAXB, counts).astype(jnp.int32)


def levels(rng, dims, pieces, least, top_value):
    def one(dim, blocks):
        heights = jax.random.uniform(jax.random.fold_in(jax.random.fold_in(rng, 6), dim), (blocks,), jnp.float32, least / len(pieces), top_value / len(pieces))
        return jnp.repeat(jnp.exp(heights), dims[dim] // blocks).reshape((-1,) + (1,) * (len(dims) - dim - 1))

    loudness = one(*pieces[0])
    for cut in pieces[1:]:
        loudness = loudness * one(*cut)
    return loudness


def scatter_about(rng, shape, scale, most, pieces=(), held_as=jnp.bfloat16):
    drawn = jax.random.normal(rng, shape, jnp.float32) * scale
    if len(pieces) > 0:
        drawn = levels(rng, shape, pieces, -0.22, 0.18) * drawn
    return jnp.clip(drawn, min=-most, max=most).astype(held_as)


def setup_inputs(seed: int = 0) -> dict:
    key_list = jax.random.split(jax.random.key(seed), 9)
    node_features = scatter_about(key_list[0], (NODES, FIN), 1.0, 6.0, ((0, 256),))
    self_weight = scatter_about(key_list[1], (FIN, FO), FIN ** -0.5, 0.21875)
    neigh_weight = scatter_about(key_list[2], (FIN, FO), FIN ** -0.5, 0.21875)
    bias = scatter_about(key_list[3], (FO,), 1.0, 4.0, (), jnp.float32)
    block_values = draw_block_values(jax.random.fold_in(key_list[8], 71), 0)
    block_coords = draw_block_coords(jax.random.fold_in(key_list[8], 71), 0)
    block_counts = draw_block_counts(jax.random.fold_in(key_list[8], 71), 0)
    out_grad = scatter_about(key_list[7], (NODES, FO), 1.0, 6.0, ((0, 256),))
    return {"node_features": node_features, "self_weight": self_weight, "neigh_weight": neigh_weight, "bias": bias, "block_values": block_values, "block_coords": block_coords, "block_counts": block_counts, "out_grad": out_grad}


def tile_term(values, coords, count, blocks, flipped):
    if flipped:
        source = coords[:, 0]
        target = coords[:, 1]
        formula = 'blk,blf->bkf'
    else:
        source = coords[:, 1]
        target = coords[:, 0]
        formula = 'bkl,blf->bkf'
    picked = blocks[source]
    product = jnp.einsum(formula, values.astype(jnp.float32), picked.astype(jnp.float32))
    live = jnp.arange(values.shape[0], dtype=jnp.int32) < count
    slots = jnp.arange(blocks.shape[0], dtype=jnp.int32)
    placing = ((target[:, None] == slots[None, :]) & live[:, None]).astype(jnp.float32)
    return jnp.einsum('bp,bkf->pkf', placing, product, precision=lax.Precision.HIGHEST)


def reference(node_features, self_weight, neigh_weight, bias, block_values, block_coords, block_counts, out_grad):
    scale = float(NODES) ** -0.5
    width = self_weight.shape[1]
    transformed = jnp.dot(node_features, neigh_weight, preferred_element_type=jnp.float32).astype(jnp.bfloat16)
    trans_blocks = transformed.reshape(SLABS, BR, BLK, width)

    def row_sum(slab_row):
        def add_tile(slab_col, total):
            return total + tile_term(block_values[slab_row, slab_col], block_coords[slab_row, slab_col], block_counts[slab_row, slab_col], trans_blocks[slab_col], False)
        return lax.fori_loop(0, SLABS, add_tile, jnp.zeros((BR, BLK, width), jnp.float32))

    aggregate = lax.map(row_sum, jnp.arange(SLABS, dtype=jnp.int32)).reshape(NODES, width)
    pre = jnp.dot(node_features, self_weight, preferred_element_type=jnp.float32) + aggregate + bias
    sigma = jax.nn.sigmoid(pre)
    activations = (pre * sigma).astype(jnp.bfloat16)
    pre_grad = (out_grad.astype(jnp.float32) * sigma * (1.0 + pre * (1.0 - sigma))).astype(jnp.bfloat16)
    grad_blocks = pre_grad.reshape(SLABS, BR, BLK, width)

    def col_sum(slab_col):
        def add_tile(slab_row, total):
            return total + tile_term(block_values[slab_row, slab_col], block_coords[slab_row, slab_col], block_counts[slab_row, slab_col], grad_blocks[slab_row], True)
        return lax.fori_loop(0, SLABS, add_tile, jnp.zeros((BR, BLK, width), jnp.float32))

    hidden = lax.map(col_sum, jnp.arange(SLABS, dtype=jnp.int32)).reshape(NODES, width).astype(jnp.bfloat16)
    feature_grad = (jnp.dot(pre_grad, self_weight.T, preferred_element_type=jnp.float32) + jnp.dot(hidden, neigh_weight.T, preferred_element_type=jnp.float32)).astype(jnp.bfloat16)
    self_grad = jnp.dot(node_features.T, pre_grad, preferred_element_type=jnp.float32) * scale
    neigh_grad = jnp.dot(node_features.T, hidden, preferred_element_type=jnp.float32) * scale
    bias_grad = jnp.sum(pre_grad.astype(jnp.float32), axis=0) * scale
    return activations, feature_grad, self_grad, neigh_grad, bias_grad
```

```python
import jax
import jax.numpy as jnp
from jax import lax
from jax.experimental import pallas as pl
from jax.experimental.pallas import tpu as pltpu
from jax.sharding import PartitionSpec as P

MESH = pl.DeviceIdType.MESH
BF16 = jnp.bfloat16
F32 = jnp.float32
FIN, FO, BLK, SLOTS, TILES = 768, 256, 128, 8, 4
ROWS, REPS, NZ, CHIPS = 32, 8, 8, 16
PIECE = FIN // CHIPS
HALF = FO // 2
NODES = ROWS * REPS * BLK


def wait_for(ref, sem):
    pltpu.make_async_copy(ref, ref, sem).wait()


def kernel(
    x_ref, ws_ref, wn_ref, bias_ref, a_ref, coords_ref, counts_ref, og_ref,
    act_ref, fg_ref, sg_ref, ng_ref, bg_ref,
    codes, merged, dense, feats, own, acc, psend, precv, selfpre,
    halves, sibrecv, pieces, piecerecv, vown, vrecv, full, bown, brecv,
    zrecv, xrecv, crecv, asend, zsend, xsend, csend, rssend, rsrecv,
    s1send, s1recv, r1send, r1recv, p1send, p1recv, g1send, g1recv, s2send, s2recv, bsend, bread,
):
    row = lax.axis_index("row")
    rep = lax.axis_index("rep")
    core = lax.rem(row, 2)
    chip = lax.div(row, 2)
    z = lax.rem(chip, NZ)
    xlo = lax.div(chip, NZ)
    col = 2 * xlo + core

    def row_at(xl, zz, cc):
        return (xl * NZ + zz) * 2 + cc

    up = row_at(xlo, lax.rem(z + 1, NZ), core)
    down = row_at(xlo, lax.rem(z + NZ - 1, NZ), core)
    across = row_at(1 - xlo, z, core)
    sibling = row_at(xlo, z, 1 - core)
    far_row = TILES * rep + lax.rem(row, TILES)
    far_rep = lax.div(row, TILES)
    is_far = far_rep != rep

    barrier = pltpu.get_barrier_semaphore()

    def greet(to_row, to_rep):
        pl.semaphore_signal(barrier, inc=1, device_id=(to_row, to_rep), device_id_type=MESH)

    lax.fori_loop(1, REPS, lambda d, _: greet(row, lax.rem(rep + d, REPS)), None)
    lax.fori_loop(1, CHIPS, lambda d, _: greet(2 * lax.rem(chip + d, CHIPS) + core, rep), None)
    greet(sibling, rep)

    @pl.when(is_far)
    def _():
        greet(far_row, far_rep)

    own[0] = jnp.dot(x_ref[...], wn_ref[...], preferred_element_type=F32).astype(BF16)

    pl.semaphore_wait(barrier, REPS - 1 + CHIPS - 1 + 1 + jnp.where(is_far, 1, 0))

    def block_of(which, zz, cc):
        return feats.at[which, zz, pl.ds(pl.multiple_of(cc * BLK, BLK), BLK), :]

    def remote(src, dst, ssem, rsem, to_row, to_rep):
        return pltpu.make_async_remote_copy(
            src_ref=src, dst_ref=dst, send_sem=ssem, recv_sem=rsem,
            device_id=(to_row, to_rep), device_id_type=MESH,
        )

    def swap_own(which):
        far_chip = lax.div(far_row, 2)
        far_col = 2 * lax.div(far_chip, NZ) + lax.rem(far_row, 2)

        @pl.when(is_far)
        def _():
            remote(
                own.at[which], block_of(which, lax.rem(far_chip, NZ), far_col),
                asend.at[which], zrecv.at[which, 0], far_row, far_rep,
            ).start()

        @pl.when(jnp.logical_not(is_far))
        def _():
            feats[which, z, pl.ds(pl.multiple_of(col * BLK, BLK), BLK), :] = own[which]

    def group_at(event):
        hops = (event + 1) // 2
        return lax.rem(z + (NZ - hops if event % 2 else hops), NZ)

    def add_group(event, which):
        zz = group_at(event)

        def chunk(i, _):
            rows = pl.ds(pl.multiple_of(i * 256, 256), 256)
            part = jnp.dot(dense[zz, rows, :], feats[which, zz], preferred_element_type=F32)
            if event == 0:
                acc[rows, :] = part
            else:
                acc[rows, :] += part
            return None

        lax.fori_loop(0, 4, chunk, None)

    def gather(which, hooks):
        def forward(event, cc, sem_index):
            block = block_of(which, group_at(event), cc)
            remote(block, block, csend.at[which], crecv.at[which, sem_index], sibling, rep).start()

        def finish(event):
            for cc in (0, 1):
                block = block_of(which, group_at(event), 2 * cc)
                wait_for(block, crecv.at[which, 2 * event + cc])
            add_group(event, which)

        for event in range(NZ):
            block = block_of(which, group_at(event), col)
            if event == 0:
                @pl.when(is_far)
                def _():
                    wait_for(block, zrecv.at[which, 0])
            else:
                wait_for(block, zrecv.at[which, event])
            if event == 0 or (event % 2 and event < 7):
                later = 1 if event == 0 else event + 2
                remote(block, block, zsend.at[which], zrecv.at[which, later], up, rep).start()
            if event % 2 == 0 and event < 6:
                remote(block, block, zsend.at[which], zrecv.at[which, event + 2], down, rep).start()
            remote(block, block, xsend.at[which], xrecv.at[which, event], across, rep).start()
            forward(event, col, 2 * event)
            if event == 0:
                hooks.get("first", lambda: None)()
            if event >= 1:
                wait_for(block, xrecv.at[which, event - 1])
                forward(event - 1, 2 * (1 - xlo) + core, 2 * event - 1)
            if event >= 2:
                finish(event - 2)
            hooks.get(event, lambda: None)()
        wait_for(block, xrecv.at[which, NZ - 1])
        forward(NZ - 1, 2 * (1 - xlo) + core, 2 * NZ - 1)
        finish(NZ - 2)
        finish(NZ - 1)

    def scatter(which, beside):
        psend[which] = acc[...].astype(BF16).reshape(REPS, BLK, FO)

        def send(d, _):
            to = lax.rem(rep + d, REPS)
            remote(
                psend.at[which, to], precv.at[which, rep], rssend.at[which], rsrecv.at[which], row, to
            ).start()

        lax.fori_loop(1, REPS, send, None)
        beside()
        total = acc[pl.ds(pl.multiple_of(rep * BLK, BLK), BLK), :]
        wait_for(precv.at[which, pl.ds(0, REPS - 1)], rsrecv.at[which])
        for d in range(1, REPS):
            total += precv[which, lax.rem(rep + d, REPS)].astype(F32)
        return total

    def grad_start(a, left, right):
        part = lax.dot_general(left, right, (((0,), (0,)), ((), ())), preferred_element_type=F32)
        halves[a, 0] = part[:, :HALF].astype(BF16)
        halves[a, 1] = part[:, HALF:].astype(BF16)
        remote(halves.at[a, 1 - core], sibrecv.at[a], s1send.at[a], s1recv.at[a], sibling, rep).start()

    def grad_chips(a):
        wait_for(sibrecv.at[a], s1recv.at[a])
        both = halves[a, core].astype(F32) + sibrecv[a].astype(F32)
        pieces[a] = both.astype(BF16).reshape(CHIPS, PIECE, HALF)

        def send(d, _):
            to = lax.rem(chip + d, CHIPS)
            remote(
                pieces.at[a, to], piecerecv.at[a, chip], r1send.at[a], r1recv.at[a], 2 * to + core, rep
            ).start()

        lax.fori_loop(1, CHIPS, send, None)

    def grad_reps(a):
        total = pieces[a, chip].astype(F32)
        wait_for(piecerecv.at[a, pl.ds(0, CHIPS - 1)], r1recv.at[a])
        for d in range(1, CHIPS):
            total += piecerecv[a, lax.rem(chip + d, CHIPS)].astype(F32)
        vown[a] = total

        def send(d, _):
            remote(
                vown.at[a], vrecv.at[a, rep], p1send.at[a], p1recv.at[a], row, lax.rem(rep + d, REPS)
            ).start()

        lax.fori_loop(1, REPS, send, None)

    def grad_hand_out(a):
        wait_for(vrecv.at[a, pl.ds(0, REPS - 1)], p1recv.at[a])
        vrecv[a, rep] = vown[a]
        total = vrecv[a, 0]
        for q in range(1, REPS):
            total += vrecv[a, q]
        full[a, core, chip] = total.astype(BF16)

        def send(d, _):
            piece = full.at[a, core, chip]
            to = lax.rem(chip + d, CHIPS)
            remote(piece, piece, g1send.at[a], g1recv.at[a], 2 * to + core, rep).start()

        lax.fori_loop(1, CHIPS, send, None)

    def grad_share(a):
        wait_for(full.at[a, core, pl.ds(0, CHIPS - 1)], g1recv.at[a])
        half = full.at[a, core]
        remote(half, half, s2send.at[a], s2recv.at[a], sibling, rep).start()

    def grad_end(a, out_ref):
        wait_for(full.at[a, 1 - core], s2recv.at[a])
        for h in (0, 1):
            out_ref[:, h * HALF:(h + 1) * HALF] = full[a, h].reshape(FIN, HALF).astype(F32) * (NODES ** -0.5)

    def grad_drain(a):
        wait_for(sibrecv.at[a], s1send.at[a])
        wait_for(piecerecv.at[a, pl.ds(0, CHIPS - 1)], r1send.at[a])
        wait_for(vrecv.at[a, pl.ds(0, REPS - 1)], p1send.at[a])
        wait_for(full.at[a, core, pl.ds(0, CHIPS - 1)], g1send.at[a])
        wait_for(full.at[a, core], s2send.at[a])

    def lay_out_strip():
        def merge(k, _):
            for b in range(SLOTS):
                where = coords_ref[0, k, b, 0] * SLOTS + coords_ref[0, k, b, 1]
                codes[k * SLOTS + b] = jnp.where(b < counts_ref[0, k], where, 255)
            for b in range(SLOTS):
                total = a_ref[0, k, b].astype(F32)
                for other in range(b):
                    same = codes[k * SLOTS + other] == codes[k * SLOTS + b]
                    total += a_ref[0, k, other].astype(F32) * jnp.where(same, 1.0, 0.0)
                merged[k, b] = total.astype(BF16)
            merged[k, SLOTS] = jnp.zeros((BLK, BLK), BF16)
            return None

        lax.fori_loop(0, TILES, merge, None)

        def place(zz, _):
            for cc in range(4):
                k = 2 * lax.rem(zz, 2) + cc % 2
                q = 4 * (cc // 2) + lax.div(zz, 2)
                for i in range(SLOTS):
                    slot = SLOTS
                    for b in range(SLOTS):
                        slot = jnp.where(codes[k * SLOTS + b] == i * SLOTS + q, b, slot)
                    dense[zz, i * BLK:(i + 1) * BLK, cc * BLK:(cc + 1) * BLK] = merged[k, slot]
            return None

        lax.fori_loop(0, NZ, place, None)

    def while_swapping():
        lay_out_strip()
        selfpre[...] = jnp.dot(x_ref[...], ws_ref[...], preferred_element_type=F32) + bias_ref[...]

    swap_own(0)
    gather(0, {"first": while_swapping})
    pre = selfpre[...] + scatter(0, lambda: None)
    sigma = jax.nn.sigmoid(pre)
    act_ref[...] = (pre * sigma).astype(BF16)
    own[1] = (og_ref[...].astype(F32) * sigma * (1.0 + pre * (1.0 - sigma))).astype(BF16)
    swap_own(1)
    grad_start(0, x_ref[...], own[1])

    gather(1, {
        "first": lambda: grad_chips(0),
        4: lambda: grad_reps(0),
        7: lambda: grad_hand_out(0),
    })

    def bias_part():
        total = jnp.zeros((8, FO), F32)
        ones = jnp.ones((8, 4 * BLK), BF16)
        for zz in range(NZ):
            total += jnp.dot(ones, feats[1, zz], preferred_element_type=F32)
        bown[...] = total

        def send(d, _):
            remote(bown, brecv.at[rep], bsend, bread, row, lax.rem(rep + d, REPS)).start()

        lax.fori_loop(1, REPS, send, None)
        grad_share(0)

    hidden = scatter(1, bias_part).astype(BF16)
    grad_start(1, x_ref[...], hidden)
    last = (((1,), (1,)), ((), ()))
    fg_ref[...] = (
        lax.dot_general(own[1], ws_ref[...], last, preferred_element_type=F32)
        + lax.dot_general(hidden, wn_ref[...], last, preferred_element_type=F32)
    ).astype(BF16)
    grad_chips(1)
    wait_for(brecv.at[pl.ds(0, REPS - 1)], bread)
    brecv[rep] = bown[...]
    total = brecv[0, 0:1, :]
    for q in range(1, REPS):
        total += brecv[q, 0:1, :]
    bg_ref[...] = total * (NODES ** -0.5)
    grad_end(0, sg_ref)
    grad_reps(1)
    grad_hand_out(1)
    for which in (0, 1):
        @pl.when(is_far)
        def _():
            wait_for(own.at[which], asend.at[which])

        wait_for(feats.at[which, pl.ds(0, 7), pl.ds(0, BLK), :], zsend.at[which])
        wait_for(feats.at[which, :, pl.ds(0, BLK), :], xsend.at[which])
        wait_for(feats.at[which, :, pl.ds(0, 2 * BLK), :], csend.at[which])
        wait_for(psend.at[which, pl.ds(0, REPS - 1)], rssend.at[which])
    wait_for(brecv.at[pl.ds(0, REPS - 1)], bsend)
    grad_drain(0)
    grad_share(1)
    grad_end(1, ng_ref)
    grad_drain(1)


def shards(node_features, self_weight, neigh_weight, bias, block_values, block_coords, block_counts, out_grad):
    vmem = pl.BlockSpec(memory_space=pltpu.VMEM)
    smem = pl.BlockSpec(memory_space=pltpu.SMEM)
    dma = pltpu.SemaphoreType.DMA
    outs = pl.pallas_call(
        kernel,
        out_shape=(
            jax.ShapeDtypeStruct((BLK, FO), BF16),
            jax.ShapeDtypeStruct((BLK, FIN), BF16),
            jax.ShapeDtypeStruct((FIN, FO), F32),
            jax.ShapeDtypeStruct((FIN, FO), F32),
            jax.ShapeDtypeStruct((1, FO), F32),
        ),
        in_specs=[vmem, vmem, vmem, vmem, vmem, smem, smem, vmem],
        out_specs=(vmem,) * 5,
        scratch_shapes=[
            pltpu.SMEM((TILES * SLOTS,), jnp.int32),
            pltpu.VMEM((TILES, SLOTS + 1, BLK, BLK), BF16),
            pltpu.VMEM((NZ, SLOTS * BLK, 4 * BLK), BF16),
            pltpu.VMEM((2, NZ, 4 * BLK, FO), BF16),
            pltpu.VMEM((2, BLK, FO), BF16),
            pltpu.VMEM((SLOTS * BLK, FO), F32),
            pltpu.VMEM((2, REPS, BLK, FO), BF16),
            pltpu.VMEM((2, REPS, BLK, FO), BF16),
            pltpu.VMEM((BLK, FO), F32),
            pltpu.VMEM((2, 2, FIN, HALF), BF16),
            pltpu.VMEM((2, FIN, HALF), BF16),
            pltpu.VMEM((2, CHIPS, PIECE, HALF), BF16),
            pltpu.VMEM((2, CHIPS, PIECE, HALF), BF16),
            pltpu.VMEM((2, PIECE, HALF), F32),
            pltpu.VMEM((2, REPS, PIECE, HALF), F32),
            pltpu.VMEM((2, 2, CHIPS, PIECE, HALF), BF16),
            pltpu.VMEM((8, FO), F32),
            pltpu.VMEM((REPS, 8, FO), F32),
            dma((2, NZ)), dma((2, NZ)), dma((2, 2 * NZ)),
            dma((2,)), dma((2,)), dma((2,)), dma((2,)), dma((2,)), dma((2,)),
            dma((2,)), dma((2,)), dma((2,)), dma((2,)), dma((2,)),
            dma((2,)), dma((2,)), dma((2,)), dma((2,)), dma((2,)),
            dma, dma,
        ],
        compiler_params=pltpu.CompilerParams(
            collective_id=0, has_side_effects=True, vmem_limit_bytes=48 * 1024 * 1024
        ),
        cost_estimate=pl.CostEstimate(flops=5 * 10 ** 9, bytes_accessed=6 * 10 ** 6, transcendentals=BLK * FO),
        name="sage_layer",
    )(
        node_features, self_weight, neigh_weight, bias.reshape(1, FO), block_values, block_coords, block_counts,
        out_grad,
    )
    return outs[:4] + (outs[4].reshape(FO),)


def solution(mesh):
    nodes = P(("row", "rep"), None)
    placed = (
        nodes, P(), P(), P(), P("row", "rep", None, None, None), P("row", "rep", None, None), P("row", "rep"), nodes,
    )
    return jax.shard_map(
        shards, mesh=mesh, in_specs=placed, out_specs=(nodes, nodes, P(), P(), P()), check_vma=False
    )
```

```python
import jax
import jax.numpy as jnp
from jax import lax
from jax.experimental import pallas as pl
from jax.experimental.pallas import tpu as pltpu
from jax.sharding import PartitionSpec as P

MESH = pl.DeviceIdType.MESH
BF16 = jnp.bfloat16
F32 = jnp.float32
FIN, FO, BLK, SLOTS, TILES = 768, 256, 128, 8, 4
ROWS, REPS, NY, NZ, CHIPS = 32, 8, 4, 8, 16
HALF = FO // 2
CHUNK = FIN // REPS
PIECE = 16
OWNERS = CHUNK // PIECE
NODES = ROWS * REPS * BLK
Z_STEP = ((0, 1), (0, -1), (1, 1), (1, -1), (0, 2), (0, -2))


def wait_for(ref, sem):
    pltpu.make_async_copy(ref, ref, sem).wait()


def kernel(
    x_hbm, ws_hbm, wn_hbm, bias_hbm, a_hbm, coords_ref, counts_ref, og_hbm,
    act_ref, fg_ref, sg_ref, ng_ref, bg_ref,
    x_ref, ws_ref, wn_ref, bias_ref, a_ref, og_ref, insem,
    codes, merged, dense, units, own, acc, psend, precv, selfpre,
    halves, sibrecv, chunks, chunkrecv, pieces, piecerecv, full, bown, brecv,
    arecv, urecv, crecv, asend, xsend, zsend, dsend, csend, rssend, rsrecv,
    s1send, s1recv, p1send, p1recv, r1send, r1recv, g1send, g1recv, q1send, q1recv, s2send, s2recv, bsend, bread,
):
    row = lax.axis_index("row")
    rep = lax.axis_index("rep")
    core = lax.rem(row, 2)
    chip = lax.div(row, 2)
    z = lax.rem(chip, NZ)
    xlo = lax.div(chip, NZ)
    xhi = lax.div(rep, NY)
    y = lax.rem(rep, NY)

    def row_at(xl, zz, cc):
        return (xl * NZ + zz) * 2 + cc

    def around(zz):
        return lax.rem(zz + 2 * NZ, NZ)

    across = row_at(1 - xlo, z, core)
    sibling = row_at(xlo, z, 1 - core)

    home = around(z + 2 * y)
    goal_rep = xlo * NY + lax.div(z, 2)
    origin_z = 2 * y + lax.rem(z, 2)

    def goal(k, h):
        return row_at(xhi, around(home + 4 * k), h)

    def origin(k, cc):
        return row_at(xhi, origin_z, cc), xlo * NY + lax.rem(lax.div(around(z - 4 * k - origin_z), 2), NY)

    def elsewhere(to_row, to_rep):
        return jnp.logical_or(to_row != row, to_rep != rep)

    barrier = pltpu.get_barrier_semaphore()

    def greet(to_row, to_rep):
        pl.semaphore_signal(barrier, inc=1, device_id=(to_row, to_rep), device_id_type=MESH)

    lax.fori_loop(1, REPS, lambda d, _: greet(row, lax.rem(rep + d, REPS)), None)
    lax.fori_loop(1, CHIPS, lambda d, _: greet(2 * lax.rem(chip + d, CHIPS) + core, rep), None)
    greet(sibling, rep)
    goals = 0
    for k in (0, 1):
        for h in (0, 1):
            from_row, from_rep = origin(k, h)

            @pl.when(elsewhere(from_row, from_rep))
            def _():
                greet(from_row, from_rep)

            goals += jnp.where(elsewhere(goal(k, h), goal_rep), 1, 0)

    inputs = [
        pltpu.make_async_copy(src, dst, insem.at[i])
        for i, (src, dst) in enumerate((
            (x_hbm, x_ref), (wn_hbm, wn_ref), (a_hbm, a_ref), (ws_hbm, ws_ref), (og_hbm, og_ref), (bias_hbm, bias_ref),
        ))
    ]
    for copy in inputs:
        copy.start()
    for copy in inputs[:2]:
        copy.wait()

    def keep(which, value):
        own[which, 0] = value[:, :HALF]
        own[which, 1] = value[:, HALF:]

    keep(0, jnp.dot(x_ref[...], wn_ref[...], preferred_element_type=F32).astype(BF16))

    pl.semaphore_wait(barrier, REPS - 1 + CHIPS - 1 + 1 + goals)

    def remote(src, dst, ssem, rsem, to_row, to_rep):
        return pltpu.make_async_remote_copy(
            src_ref=src, dst_ref=dst, send_sem=ssem, recv_sem=rsem,
            device_id=(to_row, to_rep), device_id_type=MESH,
        )

    def swap_own(which):
        place = pl.ds(pl.multiple_of(core * BLK, BLK), BLK)
        for k in (0, 1):
            for h in (0, 1):
                far = elsewhere(goal(k, h), goal_rep)

                @pl.when(far)
                def _():
                    remote(
                        own.at[which, h], units.at[which, h, xhi, home, place, :],
                        asend.at[which, 2 * k + h], arecv.at[which, 2 * k + core], goal(k, h), goal_rep,
                    ).start()

                @pl.when(jnp.logical_not(far))
                def _():
                    units[which, h, xhi, home, place, :] = own[which, h]

    def column(peer):
        return 1 - xlo if peer else xlo

    def gather(which, hooks):
        def unit(peer, offset, h):
            return units.at[which, h, column(peer), around(z + offset)]

        def arrival(peer, offset):
            return urecv.at[which, 8 * peer + offset % NZ]

        def share(peer, offset):
            piece = unit(peer, offset, core)
            remote(piece, piece, csend.at[which], crecv.at[which, 8 * peer + offset % NZ], sibling, rep).start()

        def step_z(peer, sem):
            for held, distance in Z_STEP:
                piece = unit(peer, 4 * held, core)
                to = row_at(xlo, around(z + distance), core)
                remote(piece, piece, sem, arrival(peer, 4 * held - distance), to, rep).start()

        def step_x(offset, sem):
            piece = unit(0, offset, core)
            remote(piece, piece, sem, arrival(1, offset), across, rep).start()

        first = [True]

        def add_unit(peer, offset):
            wait_for(unit(peer, offset, core), crecv.at[which, 8 * peer + offset % NZ])
            both = jnp.concatenate([unit(peer, offset, 0)[...], unit(peer, offset, 1)[...]], axis=1)
            part = jnp.dot(dense[column(peer), around(z + offset)], both, preferred_element_type=F32)
            if first[0]:
                acc[...] = part
            else:
                acc[...] += part
            first[0] = False

        def hook(name):
            hooks.get(name, lambda: None)()

        for k in (0, 1):
            for cc in (0, 1):
                @pl.when(elsewhere(*origin(k, cc)))
                def _():
                    wait_for(own.at[which, 0], arecv.at[which, 2 * k + cc])
        step_x(0, xsend.at[which])
        step_x(4, xsend.at[which])
        step_z(0, zsend.at[which])
        share(0, 0)
        share(0, 4)
        hook("swapped")
        for offset in (0, 4):
            wait_for(unit(1, offset, core), arrival(1, offset))

        @pl.when(core == 0)
        def _():
            step_z(1, dsend.at[which])

        share(1, 0)
        share(1, 4)
        offsets = [4 * held - distance for held, distance in Z_STEP]
        for offset in offsets:
            wait_for(unit(0, offset, core), arrival(0, offset))

            @pl.when(core == 1)
            def _():
                step_x(offset, dsend.at[which])

            share(0, offset)
        hook("stepped")
        rest = [(0, 0), (0, 4), (1, 0), (1, 4)] + [(0, offset) for offset in offsets]
        for i, offset in enumerate(offsets):
            for peer, earlier in rest[2 * i:2 * i + 2]:
                add_unit(peer, earlier)
            wait_for(unit(1, offset, core), arrival(1, offset))
            share(1, offset)
        hook("gathered")
        for offset in offsets:
            add_unit(1, offset)

    def scatter(which, beside):
        psend[which] = acc[...].astype(BF16).reshape(REPS, BLK, FO)

        def send(d, _):
            to = lax.rem(rep + d, REPS)
            remote(
                psend.at[which, to], precv.at[which, rep], rssend.at[which], rsrecv.at[which], row, to
            ).start()

        lax.fori_loop(1, REPS, send, None)
        beside()
        total = acc[pl.ds(pl.multiple_of(rep * BLK, BLK), BLK), :]
        wait_for(precv.at[which, pl.ds(0, REPS - 1)], rsrecv.at[which])
        for d in range(1, REPS):
            total += precv[which, lax.rem(rep + d, REPS)].astype(F32)
        return total

    def grad_start(a, left, right):
        part = lax.dot_general(left, right, (((0,), (0,)), ((), ())), preferred_element_type=F32)
        halves[a, 0] = part[:, :HALF].astype(BF16)
        halves[a, 1] = part[:, HALF:].astype(BF16)
        remote(halves.at[a, 1 - core], sibrecv.at[a], s1send.at[a], s1recv.at[a], sibling, rep).start()

    def grad_to_reps(a):
        wait_for(sibrecv.at[a], s1recv.at[a])
        both = halves[a, core].astype(F32) + sibrecv[a].astype(F32)
        chunks[a] = both.astype(BF16).reshape(REPS, CHUNK, HALF)

        def send(d, _):
            to = lax.rem(rep + d, REPS)
            remote(chunks.at[a, to], chunkrecv.at[a, rep], p1send.at[a], p1recv.at[a], row, to).start()

        lax.fori_loop(1, REPS, send, None)

    def grad_to_plane(a):
        total = chunks[a, rep].astype(F32)
        wait_for(chunkrecv.at[a, pl.ds(0, REPS - 1)], p1recv.at[a])
        for d in range(1, REPS):
            total += chunkrecv[a, lax.rem(rep + d, REPS)].astype(F32)
        pieces[a] = total.astype(BF16).reshape(OWNERS, PIECE, HALF)

        def send(d, _):
            to = lax.rem(chip + d, CHIPS)
            owner = lax.rem(to, NZ)

            @pl.when(owner < OWNERS)
            def _():
                remote(
                    pieces.at[a, owner], piecerecv.at[a, chip], r1send.at[a], r1recv.at[a], 2 * to + core, rep
                ).start()

        lax.fori_loop(1, CHIPS, send, None)

    def grad_from_plane(a):
        @pl.when(z < OWNERS)
        def _():
            wait_for(piecerecv.at[a, pl.ds(0, CHIPS - 1)], r1recv.at[a])
            piecerecv[a, chip] = pieces[a, z]
            total = piecerecv[a, 0].astype(F32)
            for m in range(1, CHIPS):
                total += piecerecv[a, m].astype(F32)
            full[a, core, rep, z] = total.astype(BF16)

            def send(d, _):
                piece = full.at[a, core, rep, z]
                to = row_at(xlo, lax.rem(z + d, NZ), core)
                remote(piece, piece, g1send.at[a], g1recv.at[a], to, rep).start()

            lax.fori_loop(1, NZ, send, None)

    def grad_from_reps(a):
        @pl.when(z < OWNERS)
        def _():
            wait_for(full.at[a, core, rep, pl.ds(0, OWNERS - 1)], g1recv.at[a])

        @pl.when(z >= OWNERS)
        def _():
            wait_for(full.at[a, core, rep], g1recv.at[a])

        def send(d, _):
            chunk = full.at[a, core, rep]
            remote(chunk, chunk, q1send.at[a], q1recv.at[a], row, lax.rem(rep + d, REPS)).start()

        lax.fori_loop(1, REPS, send, None)

    def grad_share(a):
        wait_for(full.at[a, core, pl.ds(0, REPS - 1)], q1recv.at[a])
        half = full.at[a, core]
        remote(half, half, s2send.at[a], s2recv.at[a], sibling, rep).start()

    def grad_end(a, out_ref):
        wait_for(full.at[a, 1 - core], s2recv.at[a])
        for h in (0, 1):
            out_ref[:, h * HALF:(h + 1) * HALF] = full[a, h].reshape(FIN, HALF).astype(F32) * (NODES ** -0.5)

    def grad_drain(a):
        wait_for(sibrecv.at[a], s1send.at[a])
        wait_for(chunkrecv.at[a, pl.ds(0, REPS - 1)], p1send.at[a])

        @pl.when(z < OWNERS)
        def _():
            wait_for(piecerecv.at[a, pl.ds(0, 2 * OWNERS - 1)], r1send.at[a])
            wait_for(piecerecv.at[a, pl.ds(0, NZ - 1)], g1send.at[a])

        @pl.when(z >= OWNERS)
        def _():
            wait_for(piecerecv.at[a, pl.ds(0, 2 * OWNERS)], r1send.at[a])

        wait_for(full.at[a, core, pl.ds(0, REPS - 1)], q1send.at[a])
        wait_for(full.at[a, core], s2send.at[a])

    def lay_out_strip():
        inputs[2].wait()

        def merge(k, _):
            for b in range(SLOTS):
                where = coords_ref[0, k, b, 0] * SLOTS + coords_ref[0, k, b, 1]
                codes[k * SLOTS + b] = jnp.where(b < counts_ref[0, k], where, 255)
            for b in range(SLOTS):
                total = a_ref[0, k, b].astype(F32)
                for other in range(b):
                    same = codes[k * SLOTS + other] == codes[k * SLOTS + b]
                    total += a_ref[0, k, other].astype(F32) * jnp.where(same, 1.0, 0.0)
                merged[k, b] = total.astype(BF16)
            merged[k, SLOTS] = jnp.zeros((BLK, BLK), BF16)
            return None

        lax.fori_loop(0, TILES, merge, None)

        def place(zz, _):
            parity = lax.rem(zz, 2)
            from_y = lax.rem(lax.div(around(zz - 2 * y - parity), 2), NY)
            for xl in (0, 1):
                q = NY * xl + from_y
                for cc in (0, 1):
                    k = 2 * parity + cc
                    for i in range(SLOTS):
                        slot = SLOTS
                        for b in range(SLOTS):
                            slot = jnp.where(codes[k * SLOTS + b] == i * SLOTS + q, b, slot)
                        dense[xl, zz, i * BLK:(i + 1) * BLK, cc * BLK:(cc + 1) * BLK] = merged[k, slot]
            return None

        lax.fori_loop(0, NZ, place, None)

    swap_own(0)
    lay_out_strip()
    for copy in inputs[3:]:
        copy.wait()
    selfpre[...] = jnp.dot(x_ref[...], ws_ref[...], preferred_element_type=F32) + bias_ref[...]
    gather(0, {})
    pre = selfpre[...] + scatter(0, lambda: None)
    sigma = jax.nn.sigmoid(pre)
    pre_grad = (og_ref[...].astype(F32) * sigma * (1.0 + pre * (1.0 - sigma))).astype(BF16)
    keep(1, pre_grad)
    swap_own(1)
    act_ref[...] = (pre * sigma).astype(BF16)
    grad_start(0, x_ref[...], pre_grad)
    fg_self = lax.dot_general(pre_grad, ws_ref[...], (((1,), (1,)), ((), ())), preferred_element_type=F32)
    grad_to_reps(0)

    gather(1, {
        "swapped": lambda: grad_to_plane(0),
        "stepped": lambda: grad_from_plane(0),
        "gathered": lambda: grad_from_reps(0),
    })

    def beside_scatter():
        total = jnp.zeros((8, FO), F32)
        ones = jnp.ones((8, 2 * BLK), BF16)
        for xl in (0, 1):
            for zz in range(NZ):
                both = jnp.concatenate([units[1, 0, xl, zz], units[1, 1, xl, zz]], axis=1)
                total += jnp.dot(ones, both, preferred_element_type=F32)
        bown[...] = total

        def send(d, _):
            remote(bown, brecv.at[rep], bsend, bread, row, lax.rem(rep + d, REPS)).start()

        lax.fori_loop(1, REPS, send, None)
        grad_share(0)
        grad_end(0, sg_ref)

    hidden = scatter(1, beside_scatter).astype(BF16)
    grad_start(1, x_ref[...], hidden)
    fg_ref[...] = (
        fg_self + lax.dot_general(hidden, wn_ref[...], (((1,), (1,)), ((), ())), preferred_element_type=F32)
    ).astype(BF16)
    grad_to_reps(1)
    wait_for(brecv.at[pl.ds(0, REPS - 1)], bread)
    brecv[rep] = bown[...]
    total = brecv[0, 0:1, :]
    for q in range(1, REPS):
        total += brecv[q, 0:1, :]
    bg_ref[...] = total * (NODES ** -0.5)
    grad_to_plane(1)
    grad_from_plane(1)
    for which in (0, 1):
        for k in (0, 1):
            for h in (0, 1):
                @pl.when(elsewhere(goal(k, h), goal_rep))
                def _():
                    wait_for(own.at[which, h], asend.at[which, 2 * k + h])

        wait_for(units.at[which, 0, 0, pl.ds(0, 2)], xsend.at[which])
        wait_for(units.at[which, 0, 0, pl.ds(0, 6)], zsend.at[which])
        wait_for(units.at[which, 0, 0, pl.ds(0, 6)], dsend.at[which])
        wait_for(units.at[which, 0], csend.at[which])
        wait_for(psend.at[which, pl.ds(0, REPS - 1)], rssend.at[which])
    wait_for(brecv.at[pl.ds(0, REPS - 1)], bsend)
    grad_drain(0)
    grad_from_reps(1)
    grad_share(1)
    grad_end(1, ng_ref)
    grad_drain(1)


def shards(node_features, self_weight, neigh_weight, bias, block_values, block_coords, block_counts, out_grad):
    vmem = pl.BlockSpec(memory_space=pltpu.VMEM)
    smem = pl.BlockSpec(memory_space=pltpu.SMEM)
    hbm = pl.BlockSpec(memory_space=pltpu.HBM)
    dma = pltpu.SemaphoreType.DMA
    outs = pl.pallas_call(
        kernel,
        out_shape=(
            jax.ShapeDtypeStruct((BLK, FO), BF16),
            jax.ShapeDtypeStruct((BLK, FIN), BF16),
            jax.ShapeDtypeStruct((FIN, FO), F32),
            jax.ShapeDtypeStruct((FIN, FO), F32),
            jax.ShapeDtypeStruct((1, FO), F32),
        ),
        in_specs=[hbm, hbm, hbm, hbm, hbm, smem, smem, hbm],
        out_specs=(vmem,) * 5,
        scratch_shapes=[
            pltpu.VMEM((BLK, FIN), BF16),
            pltpu.VMEM((FIN, FO), BF16),
            pltpu.VMEM((FIN, FO), BF16),
            pltpu.VMEM((1, FO), F32),
            pltpu.VMEM((1, TILES, SLOTS, BLK, BLK), BF16),
            pltpu.VMEM((BLK, FO), BF16),
            dma((6,)),
            pltpu.SMEM((TILES * SLOTS,), jnp.int32),
            pltpu.VMEM((TILES, SLOTS + 1, BLK, BLK), BF16),
            pltpu.VMEM((2, NZ, SLOTS * BLK, 2 * BLK), BF16),
            pltpu.VMEM((2, 2, 2, NZ, 2 * BLK, HALF), BF16),
            pltpu.VMEM((2, 2, BLK, HALF), BF16),
            pltpu.VMEM((SLOTS * BLK, FO), F32),
            pltpu.VMEM((2, REPS, BLK, FO), BF16),
            pltpu.VMEM((2, REPS, BLK, FO), BF16),
            pltpu.VMEM((BLK, FO), F32),
            pltpu.VMEM((2, 2, FIN, HALF), BF16),
            pltpu.VMEM((2, FIN, HALF), BF16),
            pltpu.VMEM((2, REPS, CHUNK, HALF), BF16),
            pltpu.VMEM((2, REPS, CHUNK, HALF), BF16),
            pltpu.VMEM((2, OWNERS, PIECE, HALF), BF16),
            pltpu.VMEM((2, CHIPS, PIECE, HALF), BF16),
            pltpu.VMEM((2, 2, REPS, OWNERS, PIECE, HALF), BF16),
            pltpu.VMEM((8, FO), F32),
            pltpu.VMEM((REPS, 8, FO), F32),
            dma((2, 4)), dma((2, 2 * NZ)), dma((2, 2 * NZ)), dma((2, 4)),
            dma((2,)), dma((2,)), dma((2,)), dma((2,)), dma((2,)), dma((2,)),
            dma((2,)), dma((2,)), dma((2,)), dma((2,)), dma((2,)), dma((2,)),
            dma((2,)), dma((2,)), dma((2,)), dma((2,)), dma((2,)), dma((2,)),
            dma, dma,
        ],
        compiler_params=pltpu.CompilerParams(
            collective_id=0, has_side_effects=True, vmem_limit_bytes=56 * 1024 * 1024
        ),
        cost_estimate=pl.CostEstimate(flops=5 * 10 ** 9, bytes_accessed=6 * 10 ** 6, transcendentals=BLK * FO),
        name="sage_layer",
    )(
        node_features, self_weight, neigh_weight, bias.reshape(1, FO), block_values, block_coords, block_counts,
        out_grad,
    )
    return outs[:4] + (outs[4].reshape(FO),)


def solution(mesh):
    nodes = P(("row", "rep"), None)
    placed = (
        nodes, P(), P(), P(), P("row", "rep", None, None, None), P("row", "rep", None, None), P("row", "rep"), nodes,
    )
    return jax.shard_map(
        shards, mesh=mesh, in_specs=placed, out_specs=(nodes, nodes, P(), P(), P()), check_vma=False
    )
```

```python
import jax
import jax.numpy as jnp
from jax import lax
from jax.experimental import pallas as pl
from jax.experimental.pallas import tpu as pltpu
from jax.sharding import PartitionSpec as P

MESH = pl.DeviceIdType.MESH
BF16 = jnp.bfloat16
F32 = jnp.float32
FIN, FO, BLK, SLOTS, TILES = 768, 256, 128, 8, 4
ROWS, REPS, NY, NZ, CHIPS = 32, 8, 4, 8, 16
HALF = FO // 2
PIECE = FIN // CHIPS
NODES = ROWS * REPS * BLK
Z_STEP = ((0, 1), (0, -1), (1, 1), (1, -1), (0, 2), (0, -2))


def wait_for(ref, sem):
    pltpu.make_async_copy(ref, ref, sem).wait()


def kernel(
    x_hbm, ws_hbm, wn_hbm, bias_hbm, a_hbm, coords_ref, counts_ref, og_hbm,
    act_ref, fg_ref, full, bg_ref,
    x_ref, ws_ref, wn_ref, bias_ref, a_ref, og_ref, insem,
    codes, merged, dense, units, own, acc, psend, precv, selfpre,
    halves, sibrecv, pieces, piecerecv, ringrecv, bown, brecv,
    arecv, urecv, crecv, asend, xsend, zsend, dsend, csend, rssend, rsrecv,
    s1send, s1recv, p1send, p1recv, r1send, r1recv, q1send, q1recv, s2send, s2recv, bsend, bread,
):
    row = lax.axis_index("row")
    rep = lax.axis_index("rep")
    core = lax.rem(row, 2)
    chip = lax.div(row, 2)
    z = lax.rem(chip, NZ)
    xlo = lax.div(chip, NZ)
    xhi = lax.div(rep, NY)
    y = lax.rem(rep, NY)

    def row_at(xl, zz, cc):
        return (xl * NZ + zz) * 2 + cc

    def around(zz):
        return lax.rem(zz + 2 * NZ, NZ)

    across = row_at(1 - xlo, z, core)
    sibling = row_at(xlo, z, 1 - core)

    goal_y, odd = lax.div(z, 2), lax.rem(z, 2)
    home = around(2 * goal_y + NY * odd + lax.rem(odd + y - goal_y + NY, NY))
    goal_rep = xlo * NY + goal_y

    def goal(k, h):
        return row_at(xhi, around(home + 4 * k), h)

    def maker(zz):
        place = around(zz - 2 * y)
        parity = lax.div(place, NY)
        return parity, lax.rem(lax.rem(place, NY) - parity + y + NY, NY)

    def origin(k, cc):
        parity, from_y = maker(around(z + 4 * k))
        return row_at(xhi, 2 * y + parity, cc), xlo * NY + from_y

    def elsewhere(to_row, to_rep):
        return jnp.logical_or(to_row != row, to_rep != rep)

    barrier = pltpu.get_barrier_semaphore()

    def greet(to_row, to_rep):
        pl.semaphore_signal(barrier, inc=1, device_id=(to_row, to_rep), device_id_type=MESH)

    lax.fori_loop(1, REPS, lambda d, _: greet(row, lax.rem(rep + d, REPS)), None)
    lax.fori_loop(0, REPS, lambda to, _: greet(row_at(1 - xlo, z, core), to), None)
    lax.fori_loop(1, NZ, lambda d, _: greet(row_at(xlo, around(z + d), core), rep), None)
    greet(sibling, rep)
    goals = 0
    for k in (0, 1):
        for h in (0, 1):
            from_row, from_rep = origin(k, h)

            @pl.when(elsewhere(from_row, from_rep))
            def _():
                greet(from_row, from_rep)

            goals += jnp.where(elsewhere(goal(k, h), goal_rep), 1, 0)

    inputs = [
        pltpu.make_async_copy(src, dst, insem.at[i])
        for i, (src, dst) in enumerate((
            (x_hbm, x_ref), (wn_hbm, wn_ref), (a_hbm, a_ref), (ws_hbm, ws_ref), (og_hbm, og_ref), (bias_hbm, bias_ref),
        ))
    ]
    for copy in inputs:
        copy.start()
    for copy in inputs[:2]:
        copy.wait()

    def keep(which, value):
        own[which, 0] = value[:, :HALF]
        own[which, 1] = value[:, HALF:]

    keep(0, jnp.dot(x_ref[...], wn_ref[...], preferred_element_type=F32).astype(BF16))

    pl.semaphore_wait(barrier, REPS - 1 + REPS + NZ - 1 + 1 + goals)

    def remote(src, dst, ssem, rsem, to_row, to_rep):
        return pltpu.make_async_remote_copy(
            src_ref=src, dst_ref=dst, send_sem=ssem, recv_sem=rsem,
            device_id=(to_row, to_rep), device_id_type=MESH,
        )

    def swap_own(which):
        place = pl.ds(pl.multiple_of(core * BLK, BLK), BLK)
        for k in (0, 1):
            for h in (0, 1):
                far = elsewhere(goal(k, h), goal_rep)

                @pl.when(far)
                def _():
                    remote(
                        own.at[which, h], units.at[which, h, xhi, home, place, :],
                        asend.at[which, 2 * k + h], arecv.at[which, 2 * k + core], goal(k, h), goal_rep,
                    ).start()

                @pl.when(jnp.logical_not(far))
                def _():
                    units[which, h, xhi, home, place, :] = own[which, h]

    others = [
        lax.rem(xhi + dx, 2) * NY + lax.rem(y + dy, NY)
        for dx, dy in ((1, 2), (1, 1), (1, 3), (0, 2), (1, 0), (0, 1), (0, 3))
    ]

    layer = [
        (lax.rem(xlo + dxlo, 2), lax.rem(xhi + dxhi, 2) * NY + lax.rem(y + dy, NY))
        for dxhi, dxlo, dy in (
            (1, 0, 2), (1, 0, 1), (1, 0, 3), (1, 1, 2), (0, 1, 2), (1, 0, 0), (0, 0, 2), (1, 1, 1), (1, 1, 3),
            (0, 1, 1), (0, 1, 3), (0, 0, 1), (0, 0, 3), (1, 1, 0), (0, 1, 0),
        )
    ]
    mine = xlo * REPS + rep

    def column(peer):
        return 1 - xlo if peer else xlo

    def gather(which, hooks):
        def unit(peer, offset, h):
            return units.at[which, h, column(peer), around(z + offset)]

        def arrival(peer, offset):
            return urecv.at[which, 8 * peer + offset % NZ]

        def share(peer, offset):
            piece = unit(peer, offset, core)
            remote(piece, piece, csend.at[which], crecv.at[which, 8 * peer + offset % NZ], sibling, rep).start()

        def step_z(peer, sem):
            for held, distance in Z_STEP:
                piece = unit(peer, 4 * held, core)
                to = row_at(xlo, around(z + distance), core)
                remote(piece, piece, sem, arrival(peer, 4 * held - distance), to, rep).start()

        def step_x(offset, sem):
            piece = unit(0, offset, core)
            remote(piece, piece, sem, arrival(1, offset), across, rep).start()

        first = [True]

        def add_unit(peer, offset):
            wait_for(unit(peer, offset, core), crecv.at[which, 8 * peer + offset % NZ])
            both = jnp.concatenate([unit(peer, offset, 0)[...], unit(peer, offset, 1)[...]], axis=1)
            part = jnp.dot(dense[column(peer), around(z + offset)], both, preferred_element_type=F32)
            if first[0]:
                acc[...] = part
            else:
                acc[...] += part
            first[0] = False

        def hook(name):
            hooks.get(name, lambda: None)()

        for k in (0, 1):
            for cc in (0, 1):
                @pl.when(elsewhere(*origin(k, cc)))
                def _():
                    wait_for(own.at[which, 0], arecv.at[which, 2 * k + cc])
        step_x(0, xsend.at[which])
        step_x(4, xsend.at[which])
        step_z(0, zsend.at[which])
        share(0, 0)
        share(0, 4)
        hook("swapped")
        for offset in (0, 4):
            wait_for(unit(1, offset, core), arrival(1, offset))

        @pl.when(core == 0)
        def _():
            step_z(1, dsend.at[which])

        share(1, 0)
        share(1, 4)
        offsets = [4 * held - distance for held, distance in Z_STEP]
        for offset in offsets:
            wait_for(unit(0, offset, core), arrival(0, offset))

            @pl.when(core == 1)
            def _():
                step_x(offset, dsend.at[which])

            share(0, offset)
        hook("stepped")
        rest = [(0, 0), (0, 4), (1, 0), (1, 4)] + [(0, offset) for offset in offsets]
        for i, offset in enumerate(offsets):
            for peer, earlier in rest[2 * i:2 * i + 2]:
                add_unit(peer, earlier)
            wait_for(unit(1, offset, core), arrival(1, offset))
            share(1, offset)
        hook("gathered")
        for offset in offsets:
            add_unit(1, offset)

    def scatter(which, beside):
        psend[which] = acc[...].astype(BF16).reshape(REPS, BLK, FO)

        for to in others:
            remote(
                psend.at[which, to], precv.at[which, rep], rssend.at[which], rsrecv.at[which], row, to
            ).start()
        beside()
        total = acc[pl.ds(pl.multiple_of(rep * BLK, BLK), BLK), :]
        wait_for(precv.at[which, pl.ds(0, REPS - 1)], rsrecv.at[which])
        for other in others:
            total += precv[which, other].astype(F32)
        return total

    def grad_start(a, left, right):
        part = lax.dot_general(left, right, (((0,), (0,)), ((), ())), preferred_element_type=F32)
        halves[a, 0] = part[:, :HALF].astype(BF16)
        halves[a, 1] = part[:, HALF:].astype(BF16)
        remote(halves.at[a, 1 - core], sibrecv.at[a], s1send.at[a], s1recv.at[a], sibling, rep).start()

    def grad_to_layer(a):
        wait_for(sibrecv.at[a], s1recv.at[a])
        both = halves[a, core].astype(F32) + sibrecv[a].astype(F32)
        pieces[a] = both.astype(BF16).reshape(CHIPS, PIECE, HALF)
        for xl, to in layer:
            remote(
                pieces.at[a, xl * REPS + to], piecerecv.at[a, mine], p1send.at[a], p1recv.at[a],
                row_at(xl, z, core), to,
            ).start()

    def grad_to_ring(a):
        total = pieces[a, mine].astype(F32)
        wait_for(piecerecv.at[a, pl.ds(0, CHIPS - 1)], p1recv.at[a])
        for xl, other in layer:
            total += piecerecv[a, xl * REPS + other].astype(F32)
        ringrecv[a, z] = total.astype(BF16)
        for d in (4, 3, 5, 2, 6, 1, 7):
            place = ringrecv.at[a, z]
            to = row_at(xlo, around(z + d), core)
            remote(place, place, r1send.at[a], r1recv.at[a], to, rep).start()

    def grad_from_ring(a):
        wait_for(ringrecv.at[a, pl.ds(0, NZ - 1)], r1recv.at[a])
        total = ringrecv[a, 0].astype(F32)
        for zz in range(1, NZ):
            total += ringrecv[a, zz].astype(F32)
        full[a, core, mine] = total.astype(BF16)
        piece = full.at[a, core, mine]
        for xl, to in layer:
            remote(piece, piece, q1send.at[a], q1recv.at[a], row_at(xl, z, core), to).start()

    def grad_share(a):
        wait_for(full.at[a, core, pl.ds(0, CHIPS - 1)], q1recv.at[a])
        half = full.at[a, core]
        remote(half, half, s2send.at[a], s2recv.at[a], sibling, rep).start()

    def grad_end(a):
        wait_for(full.at[a, 1 - core], s2recv.at[a])

    def grad_drain(a):
        wait_for(sibrecv.at[a], s1send.at[a])
        wait_for(piecerecv.at[a, pl.ds(0, CHIPS - 1)], p1send.at[a])
        wait_for(ringrecv.at[a, pl.ds(0, NZ - 1)], r1send.at[a])
        wait_for(full.at[a, core, pl.ds(0, CHIPS - 1)], q1send.at[a])
        wait_for(full.at[a, core], s2send.at[a])

    def lay_out_strip():
        inputs[2].wait()

        def merge(k, _):
            for b in range(SLOTS):
                where = coords_ref[0, k, 0, b] * SLOTS + coords_ref[0, k, 1, b]
                codes[k * SLOTS + b] = jnp.where(b < counts_ref[0, k], where, 255)
            for b in range(SLOTS):
                total = a_ref[0, k, b].astype(F32)
                for other in range(b):
                    same = codes[k * SLOTS + other] == codes[k * SLOTS + b]
                    total += a_ref[0, k, other].astype(F32) * jnp.where(same, 1.0, 0.0)
                merged[k, b] = total.astype(BF16)
            merged[k, SLOTS] = jnp.zeros((BLK, BLK), BF16)
            return None

        lax.fori_loop(0, TILES, merge, None)

        def place(zz, _):
            parity, from_y = maker(zz)
            for xl in (0, 1):
                q = NY * xl + from_y
                for cc in (0, 1):
                    k = 2 * parity + cc
                    for i in range(SLOTS):
                        slot = SLOTS
                        for b in range(SLOTS):
                            slot = jnp.where(codes[k * SLOTS + b] == i * SLOTS + q, b, slot)
                        dense[xl, zz, i * BLK:(i + 1) * BLK, cc * BLK:(cc + 1) * BLK] = merged[k, slot]
            return None

        lax.fori_loop(0, NZ, place, None)

    swap_own(0)
    lay_out_strip()
    for copy in inputs[3:]:
        copy.wait()
    selfpre[...] = jnp.dot(x_ref[...], ws_ref[...], preferred_element_type=F32) + bias_ref[...]
    gather(0, {})
    pre = selfpre[...] + scatter(0, lambda: None)
    sigma = jax.nn.sigmoid(pre)
    pre_grad = (og_ref[...].astype(F32) * sigma * (1.0 + pre * (1.0 - sigma))).astype(BF16)
    keep(1, pre_grad)
    swap_own(1)
    act_ref[...] = (pre * sigma).astype(BF16)
    grad_start(0, x_ref[...], pre_grad)
    fg_self = lax.dot_general(pre_grad, ws_ref[...], (((1,), (1,)), ((), ())), preferred_element_type=F32)
    grad_to_layer(0)

    gather(1, {
        "stepped": lambda: grad_to_ring(0),
        "gathered": lambda: grad_from_ring(0),
    })

    def beside_scatter():
        total = jnp.zeros((8, FO), F32)
        ones = jnp.ones((8, 2 * BLK), BF16)
        for xl in (0, 1):
            for zz in range(NZ):
                both = jnp.concatenate([units[1, 0, xl, zz], units[1, 1, xl, zz]], axis=1)
                total += jnp.dot(ones, both, preferred_element_type=F32)
        bown[...] = total

        for to in others:
            remote(bown, brecv.at[rep], bsend, bread, row, to).start()

    hidden = scatter(1, beside_scatter).astype(BF16)
    grad_start(1, x_ref[...], hidden)
    fg_ref[...] = (
        fg_self + lax.dot_general(hidden, wn_ref[...], (((1,), (1,)), ((), ())), preferred_element_type=F32)
    ).astype(BF16)
    grad_to_layer(1)
    grad_share(0)
    wait_for(brecv.at[pl.ds(0, REPS - 1)], bread)
    brecv[rep] = bown[...]
    total = brecv[0, 0:1, :]
    for q in range(1, REPS):
        total += brecv[q, 0:1, :]
    bg_ref[...] = total
    grad_end(0)
    grad_to_ring(1)
    grad_from_ring(1)
    for which in (0, 1):
        for k in (0, 1):
            for h in (0, 1):
                @pl.when(elsewhere(goal(k, h), goal_rep))
                def _():
                    wait_for(own.at[which, h], asend.at[which, 2 * k + h])

        wait_for(units.at[which, 0, 0, pl.ds(0, 2)], xsend.at[which])
        wait_for(units.at[which, 0, 0, pl.ds(0, 6)], zsend.at[which])
        wait_for(units.at[which, 0, 0, pl.ds(0, 6)], dsend.at[which])
        wait_for(units.at[which, 0], csend.at[which])
        wait_for(psend.at[which, pl.ds(0, REPS - 1)], rssend.at[which])
    wait_for(brecv.at[pl.ds(0, REPS - 1)], bsend)
    grad_drain(0)
    grad_share(1)
    grad_end(1)
    grad_drain(1)


def finish(act_in, fg_in, full, bias_in, act_ref, fg_ref, sg_ref, ng_ref, bg_ref):
    scale = NODES ** -0.5
    for a, out_ref in enumerate((sg_ref, ng_ref)):
        for h in (0, 1):
            out_ref[:, h * HALF:(h + 1) * HALF] = full[a, h].reshape(FIN, HALF).astype(F32) * scale
    act_ref[...] = act_in[...]
    fg_ref[...] = fg_in[...]
    bg_ref[...] = bias_in[...] * scale


def shards(node_features, self_weight, neigh_weight, bias, block_values, block_coords, block_counts, out_grad):
    vmem = pl.BlockSpec(memory_space=pltpu.VMEM)
    smem = pl.BlockSpec(memory_space=pltpu.SMEM)
    hbm = pl.BlockSpec(memory_space=pltpu.HBM)
    dma = pltpu.SemaphoreType.DMA
    outs = pl.pallas_call(
        kernel,
        out_shape=(
            jax.ShapeDtypeStruct((BLK, FO), BF16),
            jax.ShapeDtypeStruct((BLK, FIN), BF16),
            jax.ShapeDtypeStruct((2, 2, CHIPS, PIECE, HALF), BF16),
            jax.ShapeDtypeStruct((1, FO), F32),
        ),
        in_specs=[hbm, hbm, hbm, hbm, hbm, smem, smem, hbm],
        out_specs=(vmem,) * 4,
        scratch_shapes=[
            pltpu.VMEM((BLK, FIN), BF16),
            pltpu.VMEM((FIN, FO), BF16),
            pltpu.VMEM((FIN, FO), BF16),
            pltpu.VMEM((1, FO), F32),
            pltpu.VMEM((1, TILES, SLOTS, BLK, BLK), BF16),
            pltpu.VMEM((BLK, FO), BF16),
            dma((6,)),
            pltpu.SMEM((TILES * SLOTS,), jnp.int32),
            pltpu.VMEM((TILES, SLOTS + 1, BLK, BLK), BF16),
            pltpu.VMEM((2, NZ, SLOTS * BLK, 2 * BLK), BF16),
            pltpu.VMEM((2, 2, 2, NZ, 2 * BLK, HALF), BF16),
            pltpu.VMEM((2, 2, BLK, HALF), BF16),
            pltpu.VMEM((SLOTS * BLK, FO), F32),
            pltpu.VMEM((2, REPS, BLK, FO), BF16),
            pltpu.VMEM((2, REPS, BLK, FO), BF16),
            pltpu.VMEM((BLK, FO), F32),
            pltpu.VMEM((2, 2, FIN, HALF), BF16),
            pltpu.VMEM((2, FIN, HALF), BF16),
            pltpu.VMEM((2, CHIPS, PIECE, HALF), BF16),
            pltpu.VMEM((2, CHIPS, PIECE, HALF), BF16),
            pltpu.VMEM((2, NZ, PIECE, HALF), BF16),
            pltpu.VMEM((8, FO), F32),
            pltpu.VMEM((REPS, 8, FO), F32),
            dma((2, 4)), dma((2, 2 * NZ)), dma((2, 2 * NZ)), dma((2, 4)),
            dma((2,)), dma((2,)), dma((2,)), dma((2,)), dma((2,)), dma((2,)),
            dma((2,)), dma((2,)), dma((2,)), dma((2,)), dma((2,)), dma((2,)),
            dma((2,)), dma((2,)), dma((2,)), dma((2,)),
            dma, dma,
        ],
        compiler_params=pltpu.CompilerParams(
            collective_id=0, has_side_effects=True, vmem_limit_bytes=56 * 1024 * 1024
        ),
        cost_estimate=pl.CostEstimate(flops=5 * 10 ** 9, bytes_accessed=6 * 10 ** 6, transcendentals=BLK * FO),
        name="sage_layer",
    )(
        node_features, self_weight, neigh_weight, bias.reshape(1, FO), block_values, block_coords.swapaxes(2, 3), block_counts,
        out_grad,
    )
    act, fg, sg, ng, bg = pl.pallas_call(
        finish,
        out_shape=(
            jax.ShapeDtypeStruct((BLK, FO), BF16),
            jax.ShapeDtypeStruct((BLK, FIN), BF16),
            jax.ShapeDtypeStruct((FIN, FO), F32),
            jax.ShapeDtypeStruct((FIN, FO), F32),
            jax.ShapeDtypeStruct((1, FO), F32),
        ),
        in_specs=[vmem] * 4,
        out_specs=(vmem,) * 5,
        compiler_params=pltpu.CompilerParams(vmem_limit_bytes=56 * 1024 * 1024),
        name="finish",
    )(*outs)
    return act, fg, sg, ng, bg.reshape(FO)


def solution(mesh):
    nodes = P(("row", "rep"), None)
    placed = (
        nodes, P(), P(), P(), P("row", "rep", None, None, None), P("row", "rep", None, None), P("row", "rep"), nodes,
    )
    return jax.shard_map(
        shards, mesh=mesh, in_specs=placed, out_specs=(nodes, nodes, P(), P(), P()), check_vma=False
    )
```

```python
import jax
import jax.numpy as jnp
from jax import lax
from jax.experimental import pallas as pl
from jax.experimental.pallas import tpu as pltpu
from jax.sharding import PartitionSpec as P

MESH = pl.DeviceIdType.MESH
BF16 = jnp.bfloat16
F32 = jnp.float32
FIN, FO, BLK, SLOTS, TILES = 768, 256, 128, 8, 4
ROWS, REPS, NY, NZ, CHIPS = 32, 8, 4, 8, 16
HALF = FO // 2
PIECE = FIN // CHIPS
NODES = ROWS * REPS * BLK
Z_STEP = ((0, 1), (0, -1), (1, 1), (1, -1), (0, 2), (0, -2))


def wait_for(ref, sem):
    pltpu.make_async_copy(ref, ref, sem).wait()


def kernel(
    x_hbm, ws_hbm, wn_hbm, bias_hbm, a_hbm, coords_ref, counts_ref, og_hbm,
    act_ref, fg_ref, full, bg_ref,
    x_ref, ws_ref, wn_ref, bias_ref, a_ref, og_ref, insem,
    codes, merged, dense, units, own, acc, psend, precv, selfpre,
    halves, sibrecv, pieces, piecerecv, ringrecv, bown, brecv, slab,
    arecv, urecv, crecv, asend, xsend, zsend, dsend, csend, rssend, rsrecv,
    s1send, s1recv, p1send, p1recv, r1send, r1recv, q1send, q1recv, s2send, s2recv, bsend, bread,
    slabsend, slabrecv,
):
    row = lax.axis_index("row")
    rep = lax.axis_index("rep")
    core = lax.rem(row, 2)
    chip = lax.div(row, 2)
    z = lax.rem(chip, NZ)
    xlo = lax.div(chip, NZ)
    xhi = lax.div(rep, NY)
    y = lax.rem(rep, NY)

    def row_at(xl, zz, cc):
        return (xl * NZ + zz) * 2 + cc

    def around(zz):
        return lax.rem(zz + 2 * NZ, NZ)

    across = row_at(1 - xlo, z, core)
    sibling = row_at(xlo, z, 1 - core)

    goal_y, odd = lax.div(z, 2), lax.rem(z, 2)
    home = around(2 * goal_y + NY * odd + lax.rem(odd + y - goal_y + NY, NY))
    goal_rep = xlo * NY + goal_y

    def goal(k, h):
        return row_at(xhi, around(home + 4 * k), h)

    def maker(zz):
        place = around(zz - 2 * y)
        parity = lax.div(place, NY)
        return parity, lax.rem(lax.rem(place, NY) - parity + y + NY, NY)

    def origin(k, cc):
        parity, from_y = maker(around(z + 4 * k))
        return row_at(xhi, 2 * y + parity, cc), xlo * NY + from_y

    def elsewhere(to_row, to_rep):
        return jnp.logical_or(to_row != row, to_rep != rep)

    barrier = pltpu.get_barrier_semaphore()

    def greet(to_row, to_rep):
        pl.semaphore_signal(barrier, inc=1, device_id=(to_row, to_rep), device_id_type=MESH)

    lax.fori_loop(1, REPS, lambda d, _: greet(row, lax.rem(rep + d, REPS)), None)
    lax.fori_loop(0, REPS, lambda to, _: greet(row_at(1 - xlo, z, core), to), None)
    lax.fori_loop(1, NZ, lambda d, _: greet(row_at(xlo, around(z + d), core), rep), None)
    greet(sibling, rep)
    goals = 0
    for k in (0, 1):
        for h in (0, 1):
            from_row, from_rep = origin(k, h)

            @pl.when(elsewhere(from_row, from_rep))
            def _():
                greet(from_row, from_rep)

            goals += jnp.where(elsewhere(goal(k, h), goal_rep), 1, 0)

    inputs = [
        pltpu.make_async_copy(src, dst, insem.at[i])
        for i, (src, dst) in enumerate((
            (x_hbm, x_ref), (wn_hbm, wn_ref), (a_hbm, a_ref), (ws_hbm, ws_ref), (og_hbm, og_ref), (bias_hbm, bias_ref),
        ))
    ]
    for copy in inputs:
        copy.start()
    for copy in inputs[:2]:
        copy.wait()

    def keep(which, value):
        own[which, 0] = value[:, :HALF]
        own[which, 1] = value[:, HALF:]

    keep(0, jnp.dot(x_ref[...], wn_ref[...], preferred_element_type=F32).astype(BF16))

    pl.semaphore_wait(barrier, REPS - 1 + REPS + NZ - 1 + 1 + goals)

    def remote(src, dst, ssem, rsem, to_row, to_rep):
        return pltpu.make_async_remote_copy(
            src_ref=src, dst_ref=dst, send_sem=ssem, recv_sem=rsem,
            device_id=(to_row, to_rep), device_id_type=MESH,
        )

    def swap_own(which):
        place = pl.ds(pl.multiple_of(core * BLK, BLK), BLK)
        for k in (0, 1):
            for h in (0, 1):
                far = elsewhere(goal(k, h), goal_rep)

                @pl.when(far)
                def _():
                    remote(
                        own.at[which, h], units.at[which, h, xhi, home, place, :],
                        asend.at[which, 2 * k + h], arecv.at[which, 2 * k + core], goal(k, h), goal_rep,
                    ).start()

                @pl.when(jnp.logical_not(far))
                def _():
                    units[which, h, xhi, home, place, :] = own[which, h]

    others = [
        lax.rem(xhi + dx, 2) * NY + lax.rem(y + dy, NY)
        for dx, dy in ((1, 2), (1, 1), (1, 3), (0, 2), (1, 0), (0, 1), (0, 3))
    ]

    layer = [
        (lax.rem(xlo + dxlo, 2), lax.rem(xhi + dxhi, 2) * NY + lax.rem(y + dy, NY))
        for dxhi, dxlo, dy in (
            (1, 0, 2), (1, 0, 1), (1, 0, 3), (1, 1, 2), (0, 1, 2), (1, 0, 0), (0, 0, 2), (1, 1, 1), (1, 1, 3),
            (0, 1, 1), (0, 1, 3), (0, 0, 1), (0, 0, 3), (1, 1, 0), (0, 1, 0),
        )
    ]
    mine = xlo * REPS + rep

    def column(peer):
        return 1 - xlo if peer else xlo

    def gather(which, hooks):
        def unit(peer, offset, h):
            return units.at[which, h, column(peer), around(z + offset)]

        def arrival(peer, offset):
            return urecv.at[which, 8 * peer + offset % NZ]

        def share(peer, offset):
            piece = unit(peer, offset, core)
            remote(piece, piece, csend.at[which], crecv.at[which, 8 * peer + offset % NZ], sibling, rep).start()

        def step_z(peer, sem):
            for held, distance in Z_STEP:
                piece = unit(peer, 4 * held, core)
                to = row_at(xlo, around(z + distance), core)
                remote(piece, piece, sem, arrival(peer, 4 * held - distance), to, rep).start()

        def step_x(offset, sem):
            piece = unit(0, offset, core)
            remote(piece, piece, sem, arrival(1, offset), across, rep).start()

        first = [True]

        def add_unit(peer, offset):
            wait_for(unit(peer, offset, core), crecv.at[which, 8 * peer + offset % NZ])
            both = jnp.concatenate([unit(peer, offset, 0)[...], unit(peer, offset, 1)[...]], axis=1)
            part = jnp.dot(dense[column(peer), around(z + offset)], both, preferred_element_type=F32)
            if first[0]:
                acc[...] = part
            else:
                acc[...] += part
            first[0] = False

        def hook(name):
            hooks.get(name, lambda: None)()

        for k in (0, 1):
            for cc in (0, 1):
                @pl.when(elsewhere(*origin(k, cc)))
                def _():
                    wait_for(own.at[which, 0], arecv.at[which, 2 * k + cc])
        step_x(0, xsend.at[which])
        step_x(4, xsend.at[which])
        step_z(0, zsend.at[which])
        share(0, 0)
        share(0, 4)
        hook("swapped")
        for offset in (0, 4):
            wait_for(unit(1, offset, core), arrival(1, offset))

        @pl.when(core == 0)
        def _():
            step_z(1, dsend.at[which])

        share(1, 0)
        share(1, 4)
        offsets = [4 * held - distance for held, distance in Z_STEP]
        for offset in offsets:
            wait_for(unit(0, offset, core), arrival(0, offset))

            @pl.when(core == 1)
            def _():
                step_x(offset, dsend.at[which])

            share(0, offset)
        hook("stepped")
        rest = [(0, 0), (0, 4), (1, 0), (1, 4)] + [(0, offset) for offset in offsets]
        for i, offset in enumerate(offsets):
            for peer, earlier in rest[2 * i:2 * i + 2]:
                add_unit(peer, earlier)
            if i >= 2:
                add_unit(1, offsets[i - 2])
            wait_for(unit(1, offset, core), arrival(1, offset))
            share(1, offset)
        hook("gathered")
        for offset in offsets[-2:]:
            add_unit(1, offset)

    def round_partial(which):
        psend[which] = acc[...].astype(BF16).reshape(REPS, BLK, FO)

    def scatter(which):
        for to in others:
            remote(
                psend.at[which, to], precv.at[which, rep], rssend.at[which], rsrecv.at[which], row, to
            ).start()

    def collect(which):
        total = acc[pl.ds(pl.multiple_of(rep * BLK, BLK), BLK), :]
        wait_for(precv.at[which, pl.ds(0, REPS - 1)], rsrecv.at[which])
        for other in others:
            total += precv[which, other].astype(F32)
        return total

    opposite = lax.rem(xhi + 1, 2) * NY + y
    beside = [xhi * NY + lax.rem(y + dy, NY) for dy in (2, 1, 3)]

    def slab_start():
        slab[rep] = x_ref[...].T
        remote(slab.at[rep], slab.at[rep], slabsend, slabrecv.at[0], row, opposite).start()

    def slab_own():
        for to in beside:
            remote(slab.at[rep], slab.at[rep], slabsend, slabrecv.at[1], row, to).start()

    def slab_other():
        wait_for(slab.at[opposite], slabrecv.at[0])
        for to in beside:
            remote(slab.at[opposite], slab.at[opposite], slabsend, slabrecv.at[2], row, to).start()

    def slab_end():
        wait_for(slab.at[pl.ds(0, NY - 1)], slabrecv.at[1])
        wait_for(slab.at[pl.ds(0, NY - 1)], slabrecv.at[2])

    def grad_start(a, part):
        halves[a, 0] = part[:, :HALF].astype(BF16)
        halves[a, 1] = part[:, HALF:].astype(BF16)
        remote(halves.at[a, 1 - core], sibrecv.at[a], s1send.at[a], s1recv.at[a], sibling, rep).start()

    def grad_to_layer(a):
        wait_for(sibrecv.at[a], s1recv.at[a])
        both = halves[a, core].astype(F32) + sibrecv[a].astype(F32)
        pieces[a] = both.astype(BF16).reshape(CHIPS, PIECE, HALF)
        for xl, to in layer:
            remote(
                pieces.at[a, xl * REPS + to], piecerecv.at[a, mine], p1send.at[a], p1recv.at[a],
                row_at(xl, z, core), to,
            ).start()

    def grad_to_ring(a):
        total = pieces[a, mine].astype(F32)
        wait_for(piecerecv.at[a, pl.ds(0, CHIPS - 1)], p1recv.at[a])
        for xl, other in layer:
            total += piecerecv[a, xl * REPS + other].astype(F32)
        ringrecv[a, z] = total.astype(BF16)
        for d in (4, 3, 5, 2, 6, 1, 7):
            place = ringrecv.at[a, z]
            to = row_at(xlo, around(z + d), core)
            remote(place, place, r1send.at[a], r1recv.at[a], to, rep).start()

    def grad_from_ring(a):
        wait_for(ringrecv.at[a, pl.ds(0, NZ - 1)], r1recv.at[a])
        total = ringrecv[a, 0].astype(F32)
        for zz in range(1, NZ):
            total += ringrecv[a, zz].astype(F32)
        full[a, core, mine] = total.astype(BF16)
        piece = full.at[a, core, mine]
        for xl, to in layer:
            remote(piece, piece, q1send.at[a], q1recv.at[a], row_at(xl, z, core), to).start()

    def grad_share(a):
        wait_for(full.at[a, core, pl.ds(0, CHIPS - 1)], q1recv.at[a])
        half = full.at[a, core]
        remote(half, half, s2send.at[a], s2recv.at[a], sibling, rep).start()

    def grad_end(a):
        wait_for(full.at[a, 1 - core], s2recv.at[a])

    def grad_drain(a):
        wait_for(sibrecv.at[a], s1send.at[a])
        wait_for(piecerecv.at[a, pl.ds(0, CHIPS - 1)], p1send.at[a])
        wait_for(ringrecv.at[a, pl.ds(0, NZ - 1)], r1send.at[a])
        wait_for(full.at[a, core, pl.ds(0, CHIPS - 1)], q1send.at[a])
        wait_for(full.at[a, core], s2send.at[a])

    def lay_out_strip():
        inputs[2].wait()

        def merge(k, _):
            for b in range(SLOTS):
                where = coords_ref[0, k, 0, b] * SLOTS + coords_ref[0, k, 1, b]
                codes[k * SLOTS + b] = jnp.where(b < counts_ref[0, k], where, 255)
            for b in range(SLOTS):
                total = a_ref[0, k, b].astype(F32)
                for other in range(b):
                    same = codes[k * SLOTS + other] == codes[k * SLOTS + b]
                    total += a_ref[0, k, other].astype(F32) * jnp.where(same, 1.0, 0.0)
                merged[k, b] = total.astype(BF16)
            merged[k, SLOTS] = jnp.zeros((BLK, BLK), BF16)
            return None

        lax.fori_loop(0, TILES, merge, None)

        def place(zz, _):
            parity, from_y = maker(zz)
            for xl in (0, 1):
                q = NY * xl + from_y
                for cc in (0, 1):
                    k = 2 * parity + cc
                    for i in range(SLOTS):
                        slot = SLOTS
                        for b in range(SLOTS):
                            slot = jnp.where(codes[k * SLOTS + b] == i * SLOTS + q, b, slot)
                        dense[xl, zz, i * BLK:(i + 1) * BLK, cc * BLK:(cc + 1) * BLK] = merged[k, slot]
            return None

        lax.fori_loop(0, NZ, place, None)

    swap_own(0)
    slab_start()
    slab_own()
    lay_out_strip()
    for copy in inputs[3:]:
        copy.wait()
    selfpre[...] = jnp.dot(x_ref[...], ws_ref[...], preferred_element_type=F32) + bias_ref[...]
    gather(0, {})
    round_partial(0)
    scatter(0)
    pre = selfpre[...] + collect(0)
    sigma = jax.nn.sigmoid(pre)
    pre_grad = (og_ref[...].astype(F32) * sigma * (1.0 + pre * (1.0 - sigma))).astype(BF16)
    keep(1, pre_grad)
    swap_own(1)
    slab_other()
    act_ref[...] = (pre * sigma).astype(BF16)
    grad_start(0, jnp.dot(slab[rep], pre_grad, preferred_element_type=F32))
    fg_self = lax.dot_general(pre_grad, ws_ref[...], (((1,), (1,)), ((), ())), preferred_element_type=F32)
    grad_to_layer(0)

    gather(1, {
        "stepped": lambda: grad_to_ring(0),
        "gathered": lambda: grad_from_ring(0),
    })
    round_partial(1)
    slab_end()

    def slab_product():
        total = jnp.zeros((FIN, FO), F32)
        for pair in range(REPS // 2):
            left = jnp.concatenate([slab[2 * pair], slab[2 * pair + 1]], axis=1)
            right = psend[1, 2 * pair:2 * pair + 2].reshape(2 * BLK, FO)
            total += jnp.dot(left, right, preferred_element_type=F32)
        return total

    grad_start(1, slab_product())
    grad_to_layer(1)
    total = jnp.zeros((8, FO), F32)
    ones = jnp.ones((8, 2 * BLK), BF16)
    for xl in (0, 1):
        for zz in range(NZ):
            both = jnp.concatenate([units[1, 0, xl, zz], units[1, 1, xl, zz]], axis=1)
            total += jnp.dot(ones, both, preferred_element_type=F32)
    bown[...] = total
    for to in others:
        remote(bown, brecv.at[rep], bsend, bread, row, to).start()
    grad_to_ring(1)
    scatter(1)
    grad_share(0)
    grad_from_ring(1)
    hidden = collect(1).astype(BF16)
    fg_ref[...] = (
        fg_self + lax.dot_general(hidden, wn_ref[...], (((1,), (1,)), ((), ())), preferred_element_type=F32)
    ).astype(BF16)
    wait_for(brecv.at[pl.ds(0, REPS - 1)], bread)
    brecv[rep] = bown[...]
    total = brecv[0, 0:1, :]
    for q in range(1, REPS):
        total += brecv[q, 0:1, :]
    bg_ref[...] = total
    grad_end(0)
    for which in (0, 1):
        for k in (0, 1):
            for h in (0, 1):
                @pl.when(elsewhere(goal(k, h), goal_rep))
                def _():
                    wait_for(own.at[which, h], asend.at[which, 2 * k + h])

        wait_for(units.at[which, 0, 0, pl.ds(0, 2)], xsend.at[which])
        wait_for(units.at[which, 0, 0, pl.ds(0, 6)], zsend.at[which])
        wait_for(units.at[which, 0, 0, pl.ds(0, 6)], dsend.at[which])
        wait_for(units.at[which, 0], csend.at[which])
        wait_for(psend.at[which, pl.ds(0, REPS - 1)], rssend.at[which])
    wait_for(brecv.at[pl.ds(0, REPS - 1)], bsend)
    wait_for(slab.at[pl.ds(0, REPS - 1)], slabsend)
    grad_drain(0)
    grad_share(1)
    grad_end(1)
    grad_drain(1)


def finish(act_in, fg_in, full, bias_in, act_ref, fg_ref, sg_ref, ng_ref, bg_ref):
    scale = NODES ** -0.5
    for a, out_ref in enumerate((sg_ref, ng_ref)):
        for h in (0, 1):
            out_ref[:, h * HALF:(h + 1) * HALF] = full[a, h].reshape(FIN, HALF).astype(F32) * scale
    act_ref[...] = act_in[...]
    fg_ref[...] = fg_in[...]
    bg_ref[...] = bias_in[...] * scale


def shards(node_features, self_weight, neigh_weight, bias, block_values, block_coords, block_counts, out_grad):
    vmem = pl.BlockSpec(memory_space=pltpu.VMEM)
    smem = pl.BlockSpec(memory_space=pltpu.SMEM)
    hbm = pl.BlockSpec(memory_space=pltpu.HBM)
    dma = pltpu.SemaphoreType.DMA
    outs = pl.pallas_call(
        kernel,
        out_shape=(
            jax.ShapeDtypeStruct((BLK, FO), BF16),
            jax.ShapeDtypeStruct((BLK, FIN), BF16),
            jax.ShapeDtypeStruct((2, 2, CHIPS, PIECE, HALF), BF16),
            jax.ShapeDtypeStruct((1, FO), F32),
        ),
        in_specs=[hbm, hbm, hbm, hbm, hbm, smem, smem, hbm],
        out_specs=(vmem,) * 4,
        scratch_shapes=[
            pltpu.VMEM((BLK, FIN), BF16),
            pltpu.VMEM((FIN, FO), BF16),
            pltpu.VMEM((FIN, FO), BF16),
            pltpu.VMEM((1, FO), F32),
            pltpu.VMEM((1, TILES, SLOTS, BLK, BLK), BF16),
            pltpu.VMEM((BLK, FO), BF16),
            dma((6,)),
            pltpu.SMEM((TILES * SLOTS,), jnp.int32),
            pltpu.VMEM((TILES, SLOTS + 1, BLK, BLK), BF16),
            pltpu.VMEM((2, NZ, SLOTS * BLK, 2 * BLK), BF16),
            pltpu.VMEM((2, 2, 2, NZ, 2 * BLK, HALF), BF16),
            pltpu.VMEM((2, 2, BLK, HALF), BF16),
            pltpu.VMEM((SLOTS * BLK, FO), F32),
            pltpu.VMEM((2, REPS, BLK, FO), BF16),
            pltpu.VMEM((2, REPS, BLK, FO), BF16),
            pltpu.VMEM((BLK, FO), F32),
            pltpu.VMEM((2, 2, FIN, HALF), BF16),
            pltpu.VMEM((2, FIN, HALF), BF16),
            pltpu.VMEM((2, CHIPS, PIECE, HALF), BF16),
            pltpu.VMEM((2, CHIPS, PIECE, HALF), BF16),
            pltpu.VMEM((2, NZ, PIECE, HALF), BF16),
            pltpu.VMEM((8, FO), F32),
            pltpu.VMEM((REPS, 8, FO), F32),
            pltpu.VMEM((REPS, FIN, BLK), BF16),
            dma((2, 4)), dma((2, 2 * NZ)), dma((2, 2 * NZ)), dma((2, 4)),
            dma((2,)), dma((2,)), dma((2,)), dma((2,)), dma((2,)), dma((2,)),
            dma((2,)), dma((2,)), dma((2,)), dma((2,)), dma((2,)), dma((2,)),
            dma((2,)), dma((2,)), dma((2,)), dma((2,)),
            dma, dma, dma, dma((3,)),
        ],
        compiler_params=pltpu.CompilerParams(
            collective_id=0, has_side_effects=True, vmem_limit_bytes=56 * 1024 * 1024
        ),
        cost_estimate=pl.CostEstimate(flops=5 * 10 ** 9, bytes_accessed=6 * 10 ** 6, transcendentals=BLK * FO),
        name="sage_layer",
    )(
        node_features, self_weight, neigh_weight, bias.reshape(1, FO), block_values, block_coords.swapaxes(2, 3), block_counts,
        out_grad,
    )
    act, fg, sg, ng, bg = pl.pallas_call(
        finish,
        out_shape=(
            jax.ShapeDtypeStruct((BLK, FO), BF16),
            jax.ShapeDtypeStruct((BLK, FIN), BF16),
            jax.ShapeDtypeStruct((FIN, FO), F32),
            jax.ShapeDtypeStruct((FIN, FO), F32),
            jax.ShapeDtypeStruct((1, FO), F32),
        ),
        in_specs=[vmem] * 4,
        out_specs=(vmem,) * 5,
        compiler_params=pltpu.CompilerParams(vmem_limit_bytes=56 * 1024 * 1024),
        name="finish",
    )(*outs)
    return act, fg, sg, ng, bg.reshape(FO)


def solution(mesh):
    nodes = P(("row", "rep"), None)
    placed = (
        nodes, P(), P(), P(), P("row", "rep", None, None, None), P("row", "rep", None, None), P("row", "rep"), nodes,
    )
    return jax.shard_map(
        shards, mesh=mesh, in_specs=placed, out_specs=(nodes, nodes, P(), P(), P()), check_vma=False
    )
```

```python
import jax
import jax.numpy as jnp
from jax import lax
from jax.experimental import pallas as pl
from jax.experimental.pallas import tpu as pltpu
from jax.sharding import PartitionSpec as P

MESH = pl.DeviceIdType.MESH
BF16 = jnp.bfloat16
F32 = jnp.float32
FIN, FO, BLK, SLOTS, TILES = 768, 256, 128, 8, 4
ROWS, REPS, NY, NZ, CHIPS = 32, 8, 4, 8, 16
HALF = FO // 2
PIECE = FIN // CHIPS
PARTS = 2
NODES = ROWS * REPS * BLK
Z_STEP = ((0, 1), (0, -1), (1, 1), (1, -1), (0, 2), (0, -2))


def wait_for(ref, sem):
    pltpu.make_async_copy(ref, ref, sem).wait()


def kernel(
    x_hbm, ws_hbm, wn_hbm, bias_hbm, a_hbm, coords_ref, counts_ref, og_hbm,
    act_ref, fg_ref, full, bg_ref,
    x_ref, ws_ref, wn_ref, bias_ref, a_ref, og_ref, insem,
    codes, merged, dense, units, own, acc, psend, precv, selfpre,
    halves, sibrecv, pieces, piecerecv, ringrecv, bown, brecv, slab,
    halfsend, halfrecv, halfsem,
    arecv, urecv, crecv, asend, xsend, zsend, dsend, csend, rssend, rsrecv,
    s1send, s1recv, p1send, p1recv, r1send, r1recv, q1send, q1recv, s2send, s2recv, bsend, bread,
    slabsend, slabrecv,
):
    row = lax.axis_index("row")
    rep = lax.axis_index("rep")
    core = lax.rem(row, 2)
    chip = lax.div(row, 2)
    z = lax.rem(chip, NZ)
    xlo = lax.div(chip, NZ)
    xhi = lax.div(rep, NY)
    y = lax.rem(rep, NY)

    def row_at(xl, zz, cc):
        return (xl * NZ + zz) * 2 + cc

    def around(zz):
        return lax.rem(zz + 2 * NZ, NZ)

    across = row_at(1 - xlo, z, core)
    sibling = row_at(xlo, z, 1 - core)

    goal_y, odd = lax.div(z, 2), lax.rem(z, 2)
    home = around(2 * goal_y + NY * odd + lax.rem(odd + y - goal_y + NY, NY))
    goal_rep = xlo * NY + goal_y

    def goal(k, h):
        return row_at(xhi, around(home + 4 * k), h)

    def maker(zz):
        place = around(zz - 2 * y)
        parity = lax.div(place, NY)
        return parity, lax.rem(lax.rem(place, NY) - parity + y + NY, NY)

    def origin(k, cc):
        parity, from_y = maker(around(z + 4 * k))
        return row_at(xhi, 2 * y + parity, cc), xlo * NY + from_y

    def elsewhere(to_row, to_rep):
        return jnp.logical_or(to_row != row, to_rep != rep)

    barrier = pltpu.get_barrier_semaphore()

    def greet(to_row, to_rep):
        pl.semaphore_signal(barrier, inc=1, device_id=(to_row, to_rep), device_id_type=MESH)

    lax.fori_loop(1, REPS, lambda d, _: greet(row, lax.rem(rep + d, REPS)), None)
    lax.fori_loop(0, REPS, lambda to, _: greet(row_at(1 - xlo, z, core), to), None)
    lax.fori_loop(1, NZ, lambda d, _: greet(row_at(xlo, around(z + d), core), rep), None)
    greet(sibling, rep)
    goals = 0
    for k in (0, 1):
        for h in (0, 1):
            from_row, from_rep = origin(k, h)

            @pl.when(elsewhere(from_row, from_rep))
            def _():
                greet(from_row, from_rep)

            goals += jnp.where(elsewhere(goal(k, h), goal_rep), 1, 0)

    inputs = [
        pltpu.make_async_copy(src, dst, insem.at[i])
        for i, (src, dst) in enumerate((
            (x_hbm, x_ref), (wn_hbm, wn_ref), (a_hbm, a_ref), (ws_hbm, ws_ref), (og_hbm, og_ref), (bias_hbm, bias_ref),
        ))
    ]
    for copy in inputs:
        copy.start()
    for copy in inputs[:2]:
        copy.wait()

    def keep(which, value):
        own[which, 0] = value[:, :HALF]
        own[which, 1] = value[:, HALF:]

    keep(0, jnp.dot(x_ref[...], wn_ref[...], preferred_element_type=F32).astype(BF16))

    pl.semaphore_wait(barrier, REPS - 1 + REPS + NZ - 1 + 1 + goals)

    def remote(src, dst, ssem, rsem, to_row, to_rep):
        return pltpu.make_async_remote_copy(
            src_ref=src, dst_ref=dst, send_sem=ssem, recv_sem=rsem,
            device_id=(to_row, to_rep), device_id_type=MESH,
        )

    def swap_own(which, columns=(0, 1)):
        place = pl.ds(pl.multiple_of(core * BLK, BLK), BLK)
        for h in columns:
            for k in (0, 1):
                far = elsewhere(goal(k, h), goal_rep)

                @pl.when(far)
                def _():
                    remote(
                        own.at[which, h], units.at[which, h, xhi, home, place, :],
                        asend.at[which, 2 * k + h], arecv.at[which, 2 * k + core], goal(k, h), goal_rep,
                    ).start()

                @pl.when(jnp.logical_not(far))
                def _():
                    units[which, h, xhi, home, place, :] = own[which, h]

    others = [
        lax.rem(xhi + dx, 2) * NY + lax.rem(y + dy, NY)
        for dx, dy in ((1, 2), (1, 1), (1, 3), (0, 2), (1, 0), (0, 1), (0, 3))
    ]

    layer = [
        (lax.rem(xlo + dxlo, 2), lax.rem(xhi + dxhi, 2) * NY + lax.rem(y + dy, NY))
        for dxhi, dxlo, dy in (
            (1, 0, 2), (1, 0, 1), (1, 0, 3), (1, 1, 2), (0, 1, 2), (1, 0, 0), (0, 0, 2), (1, 1, 1), (1, 1, 3),
            (0, 1, 1), (0, 1, 3), (0, 0, 1), (0, 0, 3), (1, 1, 0), (0, 1, 0),
        )
    ]
    mine = xlo * REPS + rep

    def column(peer):
        return 1 - xlo if peer else xlo

    def gather(which, hooks):
        def unit(peer, offset, h):
            return units.at[which, h, column(peer), around(z + offset)]

        def arrival(peer, offset):
            return urecv.at[which, 8 * peer + offset % NZ]

        def share(peer, offset):
            piece = unit(peer, offset, core)
            remote(piece, piece, csend.at[which], crecv.at[which, 8 * peer + offset % NZ], sibling, rep).start()

        def step_z(peer, sem):
            for held, distance in Z_STEP:
                piece = unit(peer, 4 * held, core)
                to = row_at(xlo, around(z + distance), core)
                remote(piece, piece, sem, arrival(peer, 4 * held - distance), to, rep).start()

        def step_x(offset, sem):
            piece = unit(0, offset, core)
            remote(piece, piece, sem, arrival(1, offset), across, rep).start()

        first = [True]

        def add_unit(peer, offset):
            wait_for(unit(peer, offset, core), crecv.at[which, 8 * peer + offset % NZ])
            both = jnp.concatenate([unit(peer, offset, 0)[...], unit(peer, offset, 1)[...]], axis=1)
            part = jnp.dot(dense[column(peer), around(z + offset)], both, preferred_element_type=F32)
            if first[0]:
                acc[...] = part
            else:
                acc[...] += part
            first[0] = False

        def hook(name):
            hooks.get(name, lambda: None)()

        for k in (0, 1):
            for cc in (0, 1):
                @pl.when(elsewhere(*origin(k, cc)))
                def _():
                    wait_for(own.at[which, 0], arecv.at[which, 2 * k + cc])
        step_x(0, xsend.at[which])
        step_x(4, xsend.at[which])
        step_z(0, zsend.at[which])
        share(0, 0)
        share(0, 4)
        hook("swapped")
        for offset in (0, 4):
            wait_for(unit(1, offset, core), arrival(1, offset))

        @pl.when(core == 0)
        def _():
            step_z(1, dsend.at[which])

        share(1, 0)
        share(1, 4)
        offsets = [4 * held - distance for held, distance in Z_STEP]
        for offset in offsets:
            wait_for(unit(0, offset, core), arrival(0, offset))

            @pl.when(core == 1)
            def _():
                step_x(offset, dsend.at[which])

            share(0, offset)
        hook("stepped")
        rest = [(0, 0), (0, 4), (1, 0), (1, 4)] + [(0, offset) for offset in offsets]
        for i, offset in enumerate(offsets):
            for peer, earlier in rest[2 * i:2 * i + 2]:
                add_unit(peer, earlier)
            if i >= 2:
                add_unit(1, offsets[i - 2])
            wait_for(unit(1, offset, core), arrival(1, offset))
            share(1, offset)
        hook("gathered")
        for offset in offsets[-2:]:
            add_unit(1, offset)

    def round_partial(which):
        psend[which] = acc[...].astype(BF16).reshape(REPS, BLK, FO)

    def scatter(which):
        for to in others:
            remote(
                psend.at[which, to], precv.at[which, rep], rssend.at[which], rsrecv.at[which], row, to
            ).start()

    def collect(which):
        total = acc[pl.ds(pl.multiple_of(rep * BLK, BLK), BLK), :]
        wait_for(precv.at[which, pl.ds(0, REPS - 1)], rsrecv.at[which])
        for other in others:
            total += precv[which, other].astype(F32)
        return total

    opposite = lax.rem(xhi + 1, 2) * NY + y
    beside = [xhi * NY + lax.rem(y + dy, NY) for dy in (2, 1, 3)]

    def slab_start():
        slab[rep] = x_ref[...].T
        remote(slab.at[rep], slab.at[rep], slabsend, slabrecv.at[0], row, opposite).start()

    def slab_own():
        for to in beside:
            remote(slab.at[rep], slab.at[rep], slabsend, slabrecv.at[1], row, to).start()

    def slab_other():
        wait_for(slab.at[opposite], slabrecv.at[0])
        for to in beside:
            remote(slab.at[opposite], slab.at[opposite], slabsend, slabrecv.at[2], row, to).start()

    def slab_end():
        wait_for(slab.at[pl.ds(0, NY - 1)], slabrecv.at[1])
        wait_for(slab.at[pl.ds(0, NY - 1)], slabrecv.at[2])

    def grad_start(a, part):
        halves[a, 0] = part[:, :HALF].astype(BF16)
        halves[a, 1] = part[:, HALF:].astype(BF16)
        remote(halves.at[a, 1 - core], sibrecv.at[a], s1send.at[a], s1recv.at[a], sibling, rep).start()

    def grad_to_layer(a):
        wait_for(sibrecv.at[a], s1recv.at[a])
        both = halves[a, core].astype(F32) + sibrecv[a].astype(F32)
        pieces[a] = both.astype(BF16).reshape(CHIPS, PIECE, HALF)
        for xl, to in layer:
            remote(
                pieces.at[a, xl * REPS + to], piecerecv.at[a, mine], p1send.at[a], p1recv.at[a],
                row_at(xl, z, core), to,
            ).start()

    def grad_to_ring(a):
        total = pieces[a, mine].astype(F32)
        wait_for(piecerecv.at[a, pl.ds(0, CHIPS - 1)], p1recv.at[a])
        for xl, other in layer:
            total += piecerecv[a, xl * REPS + other].astype(F32)
        ringrecv[a, z] = total.astype(BF16)
        for d in (4, 3, 5, 2, 6, 1, 7):
            place = ringrecv.at[a, z]
            to = row_at(xlo, around(z + d), core)
            remote(place, place, r1send.at[a], r1recv.at[a], to, rep).start()

    def grad_from_ring(a):
        wait_for(ringrecv.at[a, pl.ds(0, NZ - 1)], r1recv.at[a])
        total = ringrecv[a, 0].astype(F32)
        for zz in range(1, NZ):
            total += ringrecv[a, zz].astype(F32)
        full[a, core, mine] = total.astype(BF16)
        piece = full.at[a, core, mine]
        for xl, to in layer:
            remote(piece, piece, q1send.at[a], q1recv.at[a], row_at(xl, z, core), to).start()

    def grad_share(a):
        wait_for(full.at[a, core, pl.ds(0, CHIPS - 1)], q1recv.at[a])
        half = full.at[a, core]
        remote(half, half, s2send.at[a], s2recv.at[a], sibling, rep).start()

    def grad_end(a):
        wait_for(full.at[a, 1 - core], s2recv.at[a])

    def grad_drain(a):
        wait_for(sibrecv.at[a], s1send.at[a])
        wait_for(piecerecv.at[a, pl.ds(0, CHIPS - 1)], p1send.at[a])
        wait_for(ringrecv.at[a, pl.ds(0, NZ - 1)], r1send.at[a])
        wait_for(full.at[a, core, pl.ds(0, CHIPS - 1)], q1send.at[a])
        wait_for(full.at[a, core], s2send.at[a])

    def lay_out_strip():
        inputs[2].wait()

        def merge(k, _):
            for b in range(SLOTS):
                where = coords_ref[0, k, 0, b] * SLOTS + coords_ref[0, k, 1, b]
                codes[k * SLOTS + b] = jnp.where(b < counts_ref[0, k], where, 255)
            for b in range(SLOTS):
                total = a_ref[0, k, b].astype(F32)
                for other in range(b):
                    same = codes[k * SLOTS + other] == codes[k * SLOTS + b]
                    total += a_ref[0, k, other].astype(F32) * jnp.where(same, 1.0, 0.0)
                merged[k, b] = total.astype(BF16)
            merged[k, SLOTS] = jnp.zeros((BLK, BLK), BF16)
            return None

        lax.fori_loop(0, TILES, merge, None)

        def place(zz, _):
            parity, from_y = maker(zz)
            for xl in (0, 1):
                q = NY * xl + from_y
                for cc in (0, 1):
                    k = 2 * parity + cc
                    for i in range(SLOTS):
                        slot = SLOTS
                        for b in range(SLOTS):
                            slot = jnp.where(codes[k * SLOTS + b] == i * SLOTS + q, b, slot)
                        dense[xl, zz, i * BLK:(i + 1) * BLK, cc * BLK:(cc + 1) * BLK] = merged[k, slot]
            return None

        lax.fori_loop(0, NZ, place, None)

    swap_own(0)
    slab_start()
    slab_own()
    lay_out_strip()
    for copy in inputs[3:]:
        copy.wait()
    selfpre[...] = jnp.dot(x_ref[...], ws_ref[...], preferred_element_type=F32) + bias_ref[...]
    gather(0, {})
    half_columns = [slice(h * HALF, (h + 1) * HALF) for h in (0, 1)]
    for h, columns in enumerate(half_columns):
        halfsend[h] = acc[:, columns].astype(BF16).reshape(REPS, BLK, HALF)
        for to in others:
            remote(halfsend.at[h, to], halfrecv.at[h, rep], rssend.at[0], halfsem.at[h], row, to).start()
    pre_halves = []
    for h, columns in enumerate(half_columns):
        total = acc[pl.ds(pl.multiple_of(rep * BLK, BLK), BLK), columns] + selfpre[:, columns]
        wait_for(halfrecv.at[h, pl.ds(0, REPS - 1)], halfsem.at[h])
        for other in others:
            total += halfrecv[h, other].astype(F32)
        sigma = jax.nn.sigmoid(total)
        slope = og_ref[:, columns].astype(F32) * sigma * (1.0 + total * (1.0 - sigma))
        own[1, h] = slope.astype(BF16)
        swap_own(1, (h,))
        act_ref[:, columns] = (total * sigma).astype(BF16)
    slab_other()
    pre_grad = jnp.concatenate([own[1, 0], own[1, 1]], axis=1)
    grad_start(0, jnp.dot(slab[rep], pre_grad, preferred_element_type=F32))
    fg_self = lax.dot_general(pre_grad, ws_ref[...], (((1,), (1,)), ((), ())), preferred_element_type=F32)
    grad_to_layer(0)

    gather(1, {
        "stepped": lambda: grad_to_ring(0),
        "gathered": lambda: grad_from_ring(0),
    })
    round_partial(1)
    slab_end()

    def slab_product():
        total = jnp.zeros((FIN, FO), F32)
        for pair in range(REPS // 2):
            left = jnp.concatenate([slab[2 * pair], slab[2 * pair + 1]], axis=1)
            right = psend[1, 2 * pair:2 * pair + 2].reshape(2 * BLK, FO)
            total += jnp.dot(left, right, preferred_element_type=F32)
        return total

    grad_start(1, slab_product())
    grad_to_layer(1)
    total = jnp.zeros((8, FO), F32)
    ones = jnp.ones((8, 2 * BLK), BF16)
    for xl in (0, 1):
        for zz in range(NZ):
            both = jnp.concatenate([units[1, 0, xl, zz], units[1, 1, xl, zz]], axis=1)
            total += jnp.dot(ones, both, preferred_element_type=F32)
    bown[...] = total
    for to in others:
        remote(bown, brecv.at[rep], bsend, bread, row, to).start()
    grad_to_ring(1)
    scatter(1)
    grad_share(0)
    grad_from_ring(1)
    hidden = collect(1).astype(BF16)
    fg_ref[...] = (
        fg_self + lax.dot_general(hidden, wn_ref[...], (((1,), (1,)), ((), ())), preferred_element_type=F32)
    ).astype(BF16)
    wait_for(brecv.at[pl.ds(0, REPS - 1)], bread)
    brecv[rep] = bown[...]
    total = brecv[0, 0:1, :]
    for q in range(1, REPS):
        total += brecv[q, 0:1, :]
    bg_ref[...] = total
    grad_end(0)
    for which in (0, 1):
        for k in (0, 1):
            for h in (0, 1):
                @pl.when(elsewhere(goal(k, h), goal_rep))
                def _():
                    wait_for(own.at[which, h], asend.at[which, 2 * k + h])

        wait_for(units.at[which, 0, 0, pl.ds(0, 2)], xsend.at[which])
        wait_for(units.at[which, 0, 0, pl.ds(0, 6)], zsend.at[which])
        wait_for(units.at[which, 0, 0, pl.ds(0, 6)], dsend.at[which])
        wait_for(units.at[which, 0], csend.at[which])
        wait_for(psend.at[which, pl.ds(0, REPS - 1)], rssend.at[which])
    wait_for(brecv.at[pl.ds(0, REPS - 1)], bsend)
    wait_for(slab.at[pl.ds(0, REPS - 1)], slabsend)
    grad_drain(0)
    grad_share(1)
    grad_end(1)
    grad_drain(1)


def finish(act_in, fg_in, full, bias_in, act_ref, fg_ref, sg_ref, ng_ref, bg_ref):
    scale = NODES ** -0.5
    rows = FIN // PARTS
    for a, out_ref in enumerate((sg_ref, ng_ref)):
        for h in (0, 1):
            out_ref[:, h * HALF:(h + 1) * HALF] = full[a, h].reshape(rows, HALF).astype(F32) * scale
    act_ref[...] = act_in[...]
    fg_ref[...] = fg_in[...]
    bg_ref[...] = bias_in[...] * scale


def shards(node_features, self_weight, neigh_weight, bias, block_values, block_coords, block_counts, out_grad):
    vmem = pl.BlockSpec(memory_space=pltpu.VMEM)
    smem = pl.BlockSpec(memory_space=pltpu.SMEM)
    hbm = pl.BlockSpec(memory_space=pltpu.HBM)
    dma = pltpu.SemaphoreType.DMA
    outs = pl.pallas_call(
        kernel,
        out_shape=(
            jax.ShapeDtypeStruct((BLK, FO), BF16),
            jax.ShapeDtypeStruct((BLK, FIN), BF16),
            jax.ShapeDtypeStruct((2, 2, CHIPS, PIECE, HALF), BF16),
            jax.ShapeDtypeStruct((1, FO), F32),
        ),
        in_specs=[hbm, hbm, hbm, hbm, hbm, smem, smem, hbm],
        out_specs=(vmem,) * 4,
        scratch_shapes=[
            pltpu.VMEM((BLK, FIN), BF16),
            pltpu.VMEM((FIN, FO), BF16),
            pltpu.VMEM((FIN, FO), BF16),
            pltpu.VMEM((1, FO), F32),
            pltpu.VMEM((1, TILES, SLOTS, BLK, BLK), BF16),
            pltpu.VMEM((BLK, FO), BF16),
            dma((6,)),
            pltpu.SMEM((TILES * SLOTS,), jnp.int32),
            pltpu.VMEM((TILES, SLOTS + 1, BLK, BLK), BF16),
            pltpu.VMEM((2, NZ, SLOTS * BLK, 2 * BLK), BF16),
            pltpu.VMEM((2, 2, 2, NZ, 2 * BLK, HALF), BF16),
            pltpu.VMEM((2, 2, BLK, HALF), BF16),
            pltpu.VMEM((SLOTS * BLK, FO), F32),
            pltpu.VMEM((2, REPS, BLK, FO), BF16),
            pltpu.VMEM((2, REPS, BLK, FO), BF16),
            pltpu.VMEM((BLK, FO), F32),
            pltpu.VMEM((2, 2, FIN, HALF), BF16),
            pltpu.VMEM((2, FIN, HALF), BF16),
            pltpu.VMEM((2, CHIPS, PIECE, HALF), BF16),
            pltpu.VMEM((2, CHIPS, PIECE, HALF), BF16),
            pltpu.VMEM((2, NZ, PIECE, HALF), BF16),
            pltpu.VMEM((8, FO), F32),
            pltpu.VMEM((REPS, 8, FO), F32),
            pltpu.VMEM((REPS, FIN, BLK), BF16),
            pltpu.VMEM((2, REPS, BLK, HALF), BF16),
            pltpu.VMEM((2, REPS, BLK, HALF), BF16),
            dma((2,)),
            dma((2, 4)), dma((2, 2 * NZ)), dma((2, 2 * NZ)), dma((2, 4)),
            dma((2,)), dma((2,)), dma((2,)), dma((2,)), dma((2,)), dma((2,)),
            dma((2,)), dma((2,)), dma((2,)), dma((2,)), dma((2,)), dma((2,)),
            dma((2,)), dma((2,)), dma((2,)), dma((2,)),
            dma, dma, dma, dma((3,)),
        ],
        compiler_params=pltpu.CompilerParams(
            collective_id=0, has_side_effects=True, vmem_limit_bytes=56 * 1024 * 1024
        ),
        cost_estimate=pl.CostEstimate(flops=5 * 10 ** 9, bytes_accessed=6 * 10 ** 6, transcendentals=BLK * FO),
        name="sage_layer",
    )(
        node_features, self_weight, neigh_weight, bias.reshape(1, FO), block_values, block_coords.swapaxes(2, 3), block_counts,
        out_grad,
    )
    act, fg, sg, ng, bg = pl.pallas_call(
        finish,
        out_shape=(
            jax.ShapeDtypeStruct((BLK, FO), BF16),
            jax.ShapeDtypeStruct((BLK, FIN), BF16),
            jax.ShapeDtypeStruct((FIN, FO), F32),
            jax.ShapeDtypeStruct((FIN, FO), F32),
            jax.ShapeDtypeStruct((1, FO), F32),
        ),
        grid=(PARTS,),
        in_specs=[
            pl.BlockSpec((BLK // PARTS, FO), lambda i: (i, 0)),
            pl.BlockSpec((BLK // PARTS, FIN), lambda i: (i, 0)),
            pl.BlockSpec((2, 2, CHIPS // PARTS, PIECE, HALF), lambda i: (0, 0, i, 0, 0)),
            pl.BlockSpec((1, FO), lambda i: (0, 0)),
        ],
        out_specs=(
            pl.BlockSpec((BLK // PARTS, FO), lambda i: (i, 0)),
            pl.BlockSpec((BLK // PARTS, FIN), lambda i: (i, 0)),
            pl.BlockSpec((FIN // PARTS, FO), lambda i: (i, 0)),
            pl.BlockSpec((FIN // PARTS, FO), lambda i: (i, 0)),
            pl.BlockSpec((1, FO), lambda i: (0, 0)),
        ),
        compiler_params=pltpu.CompilerParams(vmem_limit_bytes=56 * 1024 * 1024),
        name="finish",
    )(*outs)
    return act, fg, sg, ng, bg.reshape(FO)


def solution(mesh):
    nodes = P(("row", "rep"), None)
    placed = (
        nodes, P(), P(), P(), P("row", "rep", None, None, None), P("row", "rep", None, None), P("row", "rep"), nodes,
    )
    return jax.shard_map(
        shards, mesh=mesh, in_specs=placed, out_specs=(nodes, nodes, P(), P(), P()), check_vma=False
    )
```

```python
import jax
import jax.numpy as jnp
from jax import lax
from jax.experimental import pallas as pl
from jax.experimental.pallas import tpu as pltpu
from jax.sharding import PartitionSpec as P

MESH = pl.DeviceIdType.MESH
BF16 = jnp.bfloat16
F32 = jnp.float32
FIN, FO, BLK, SLOTS, TILES = 768, 256, 128, 8, 4
ROWS, REPS, NY, NZ, CHIPS = 32, 8, 4, 8, 16
HALF = FO // 2
PIECE = FIN // CHIPS
PARTS = 2
NODES = ROWS * REPS * BLK
Z_STEP = ((0, 1), (0, -1), (1, 1), (1, -1), (0, 2), (0, -2))


def wait_for(ref, sem):
    pltpu.make_async_copy(ref, ref, sem).wait()


def kernel(
    x_hbm, ws_hbm, wn_hbm, bias_hbm, a_hbm, coords_ref, counts_ref, og_hbm,
    act_ref, fg_ref, full, bg_ref,
    x_ref, ws_ref, wn_ref, bias_ref, a_ref, og_ref, insem,
    codes, merged, dense, units, own, acc, psend, precv, selfpre,
    halves, sibrecv, pieces, piecerecv, ringrecv, bown, brecv, slab,
    halfsend, halfrecv, halfsem,
    arecv, urecv, crecv, asend, xsend, zsend, dsend, csend, rssend, rsrecv,
    s1send, s1recv, p1send, p1recv, r1send, r1recv, q1send, q1recv, s2send, s2recv, bsend, bread,
    slabsend, slabrecv,
):
    row = lax.axis_index("row")
    rep = lax.axis_index("rep")
    core = lax.rem(row, 2)
    chip = lax.div(row, 2)
    z = lax.rem(chip, NZ)
    xlo = lax.div(chip, NZ)
    xhi = lax.div(rep, NY)
    y = lax.rem(rep, NY)

    def row_at(xl, zz, cc):
        return (xl * NZ + zz) * 2 + cc

    def around(zz):
        return lax.rem(zz + 2 * NZ, NZ)

    across = row_at(1 - xlo, z, core)
    sibling = row_at(xlo, z, 1 - core)

    goal_y, odd = lax.div(z, 2), lax.rem(z, 2)
    home = around(2 * goal_y + NY * odd + lax.rem(odd + y - goal_y + NY, NY))
    goal_rep = xlo * NY + goal_y

    def goal(k, h):
        return row_at(xhi, around(home + 4 * k), h)

    def maker(zz):
        place = around(zz - 2 * y)
        parity = lax.div(place, NY)
        return parity, lax.rem(lax.rem(place, NY) - parity + y + NY, NY)

    def origin(k, cc):
        parity, from_y = maker(around(z + 4 * k))
        return row_at(xhi, 2 * y + parity, cc), xlo * NY + from_y

    def elsewhere(to_row, to_rep):
        return jnp.logical_or(to_row != row, to_rep != rep)

    inputs = [
        pltpu.make_async_copy(src, dst, insem.at[i])
        for i, (src, dst) in enumerate((
            (x_hbm, x_ref), (wn_hbm, wn_ref), (a_hbm, a_ref), (ws_hbm, ws_ref), (og_hbm, og_ref), (bias_hbm, bias_ref),
        ))
    ]
    for copy in inputs:
        copy.start()

    barrier = pltpu.get_barrier_semaphore()

    def greet(to_row, to_rep):
        pl.semaphore_signal(barrier, inc=1, device_id=(to_row, to_rep), device_id_type=MESH)

    goals = 0
    for k in (0, 1):
        for h in (0, 1):
            from_row, from_rep = origin(k, h)

            @pl.when(elsewhere(from_row, from_rep))
            def _():
                greet(from_row, from_rep)

            goals += jnp.where(elsewhere(goal(k, h), goal_rep), 1, 0)
    lax.fori_loop(1, REPS, lambda d, _: greet(row, lax.rem(rep + d, REPS)), None)
    lax.fori_loop(0, REPS, lambda to, _: greet(row_at(1 - xlo, z, core), to), None)
    lax.fori_loop(1, NZ, lambda d, _: greet(row_at(xlo, around(z + d), core), rep), None)
    greet(sibling, rep)

    for copy in inputs[:2]:
        copy.wait()

    def keep(which, value):
        own[which, 0] = value[:, :HALF]
        own[which, 1] = value[:, HALF:]

    keep(0, jnp.dot(x_ref[...], wn_ref[...], preferred_element_type=F32).astype(BF16))

    pl.semaphore_wait(barrier, REPS - 1 + REPS + NZ - 1 + 1 + goals)

    def remote(src, dst, ssem, rsem, to_row, to_rep):
        return pltpu.make_async_remote_copy(
            src_ref=src, dst_ref=dst, send_sem=ssem, recv_sem=rsem,
            device_id=(to_row, to_rep), device_id_type=MESH,
        )

    def swap_own(which, columns=(0, 1)):
        place = pl.ds(pl.multiple_of(core * BLK, BLK), BLK)
        for h in columns:
            for k in (0, 1):
                far = elsewhere(goal(k, h), goal_rep)

                @pl.when(far)
                def _():
                    remote(
                        own.at[which, h], units.at[which, h, xhi, home, place, :],
                        asend.at[which, 2 * k + h], arecv.at[which, 2 * k + core], goal(k, h), goal_rep,
                    ).start()

                @pl.when(jnp.logical_not(far))
                def _():
                    units[which, h, xhi, home, place, :] = own[which, h]

    others = [
        lax.rem(xhi + dx, 2) * NY + lax.rem(y + dy, NY)
        for dx, dy in ((1, 2), (1, 1), (1, 3), (0, 2), (1, 0), (0, 1), (0, 3))
    ]

    layer = [
        (lax.rem(xlo + dxlo, 2), lax.rem(xhi + dxhi, 2) * NY + lax.rem(y + dy, NY))
        for dxhi, dxlo, dy in (
            (1, 0, 2), (1, 0, 1), (1, 0, 3), (1, 0, 0), (0, 0, 2), (0, 0, 1), (0, 0, 3),
            (1, 1, 2), (0, 1, 2), (1, 1, 1), (1, 1, 3), (0, 1, 1), (0, 1, 3), (1, 1, 0), (0, 1, 0),
        )
    ]
    mine = xlo * REPS + rep

    def column(peer):
        return 1 - xlo if peer else xlo

    def gather(which, hooks):
        def unit(peer, offset, h):
            return units.at[which, h, column(peer), around(z + offset)]

        def arrival(peer, offset):
            return urecv.at[which, 8 * peer + offset % NZ]

        def share(peer, offset):
            piece = unit(peer, offset, core)
            remote(piece, piece, csend.at[which], crecv.at[which, 8 * peer + offset % NZ], sibling, rep).start()

        def step_z(peer, sem):
            for held, distance in Z_STEP:
                piece = unit(peer, 4 * held, core)
                to = row_at(xlo, around(z + distance), core)
                remote(piece, piece, sem, arrival(peer, 4 * held - distance), to, rep).start()

        def step_x(offset, sem):
            piece = unit(0, offset, core)
            remote(piece, piece, sem, arrival(1, offset), across, rep).start()

        first = [True]

        def add_unit(peer, offset):
            wait_for(unit(peer, offset, core), crecv.at[which, 8 * peer + offset % NZ])
            both = jnp.concatenate([unit(peer, offset, 0)[...], unit(peer, offset, 1)[...]], axis=1)
            part = jnp.dot(dense[column(peer), around(z + offset)], both, preferred_element_type=F32)
            if first[0]:
                acc[...] = part
            else:
                acc[...] += part
            first[0] = False

        def hook(name):
            hooks.get(name, lambda: None)()

        for k in (0, 1):
            for cc in (0, 1):
                @pl.when(elsewhere(*origin(k, cc)))
                def _():
                    wait_for(own.at[which, 0], arecv.at[which, 2 * k + cc])
        step_x(0, xsend.at[which])
        step_x(4, xsend.at[which])
        step_z(0, zsend.at[which])
        share(0, 0)
        share(0, 4)
        hook("swapped")
        for offset in (0, 4):
            wait_for(unit(1, offset, core), arrival(1, offset))

        @pl.when(core == 0)
        def _():
            step_z(1, dsend.at[which])

        share(1, 0)
        share(1, 4)
        offsets = [4 * held - distance for held, distance in Z_STEP]
        for offset in offsets:
            wait_for(unit(0, offset, core), arrival(0, offset))

            @pl.when(core == 1)
            def _():
                step_x(offset, dsend.at[which])

            share(0, offset)
        hook("stepped")
        rest = [(0, 0), (0, 4), (1, 0), (1, 4)] + [(0, offset) for offset in offsets]
        for i, offset in enumerate(offsets):
            for peer, earlier in rest[2 * i:2 * i + 2]:
                add_unit(peer, earlier)
            if i >= 2:
                add_unit(1, offsets[i - 2])
            wait_for(unit(1, offset, core), arrival(1, offset))
            share(1, offset)
        hook("gathered")
        for offset in offsets[-2:]:
            add_unit(1, offset)

    def round_partial(which):
        psend[which] = acc[...].astype(BF16).reshape(REPS, BLK, FO)

    def scatter(which):
        for to in others:
            remote(
                psend.at[which, to], precv.at[which, rep], rssend.at[which], rsrecv.at[which], row, to
            ).start()

    def collect(which):
        total = acc[pl.ds(pl.multiple_of(rep * BLK, BLK), BLK), :]
        wait_for(precv.at[which, pl.ds(0, REPS - 1)], rsrecv.at[which])
        for other in others:
            total += precv[which, other].astype(F32)
        return total

    opposite = lax.rem(xhi + 1, 2) * NY + y
    beside = [xhi * NY + lax.rem(y + dy, NY) for dy in (2, 1, 3)]

    def slab_start():
        slab[rep] = x_ref[...].T
        remote(slab.at[rep], slab.at[rep], slabsend, slabrecv.at[0], row, opposite).start()

    def slab_own():
        for to in beside:
            remote(slab.at[rep], slab.at[rep], slabsend, slabrecv.at[1], row, to).start()

    def slab_other():
        wait_for(slab.at[opposite], slabrecv.at[0])
        for to in beside:
            remote(slab.at[opposite], slab.at[opposite], slabsend, slabrecv.at[2], row, to).start()

    def slab_end():
        wait_for(slab.at[pl.ds(0, NY - 1)], slabrecv.at[1])
        wait_for(slab.at[pl.ds(0, NY - 1)], slabrecv.at[2])

    def rows_for(d):
        return pl.ds(pl.multiple_of(lax.rem(xlo + d, 2) * (FIN // 2), FIN // 2), FIN // 2)

    def grad_start(a, product):
        for d in (0, 1):
            rows = rows_for(d)
            part = product(rows)
            halves[a, 0, rows, :] = part[:, :HALF].astype(BF16)
            halves[a, 1, rows, :] = part[:, HALF:].astype(BF16)
            remote(
                halves.at[a, 1 - core, rows], sibrecv.at[a, rows], s1send.at[a, d], s1recv.at[a, d], sibling, rep
            ).start()

    def grad_to_layer(a):
        for d in (0, 1):
            rows = rows_for(d)
            wait_for(sibrecv.at[a, rows], s1recv.at[a, d])
            both = halves[a, core, rows, :].astype(F32) + sibrecv[a, rows, :].astype(F32)
            owned = pl.ds(pl.multiple_of(lax.rem(xlo + d, 2) * REPS, REPS), REPS)
            pieces[a, owned] = both.astype(BF16).reshape(REPS, PIECE, HALF)
            for xl, to in layer[:7] if d == 0 else layer[7:]:
                remote(
                    pieces.at[a, xl * REPS + to], piecerecv.at[a, mine], p1send.at[a], p1recv.at[a],
                    row_at(xl, z, core), to,
                ).start()

    def grad_to_ring(a):
        total = pieces[a, mine].astype(F32)
        wait_for(piecerecv.at[a, pl.ds(0, CHIPS - 1)], p1recv.at[a])
        for xl, other in layer:
            total += piecerecv[a, xl * REPS + other].astype(F32)
        ringrecv[a, z] = total.astype(BF16)
        for d in (4, 3, 5, 2, 6, 1, 7):
            place = ringrecv.at[a, z]
            to = row_at(xlo, around(z + d), core)
            remote(place, place, r1send.at[a], r1recv.at[a], to, rep).start()

    def grad_from_ring(a):
        wait_for(ringrecv.at[a, pl.ds(0, NZ - 1)], r1recv.at[a])
        total = ringrecv[a, 0].astype(F32)
        for zz in range(1, NZ):
            total += ringrecv[a, zz].astype(F32)
        full[a, core, mine] = total.astype(BF16)
        piece = full.at[a, core, mine]
        for xl, to in layer:
            remote(piece, piece, q1send.at[a], q1recv.at[a], row_at(xl, z, core), to).start()

    def grad_share(a):
        wait_for(full.at[a, core, pl.ds(0, CHIPS - 1)], q1recv.at[a])
        half = full.at[a, core]
        remote(half, half, s2send.at[a], s2recv.at[a], sibling, rep).start()

    def grad_end(a):
        wait_for(full.at[a, 1 - core], s2recv.at[a])

    def grad_drain(a):
        for d in (0, 1):
            wait_for(sibrecv.at[a, rows_for(d)], s1send.at[a, d])
        wait_for(piecerecv.at[a, pl.ds(0, CHIPS - 1)], p1send.at[a])
        wait_for(ringrecv.at[a, pl.ds(0, NZ - 1)], r1send.at[a])
        wait_for(full.at[a, core, pl.ds(0, CHIPS - 1)], q1send.at[a])
        wait_for(full.at[a, core], s2send.at[a])

    def lay_out_strip():
        inputs[2].wait()

        def merge(k, _):
            for b in range(SLOTS):
                where = coords_ref[0, k, 0, b] * SLOTS + coords_ref[0, k, 1, b]
                codes[k * SLOTS + b] = jnp.where(b < counts_ref[0, k], where, 255)
            for b in range(SLOTS):
                total = a_ref[0, k, b].astype(F32)
                for other in range(b):
                    same = codes[k * SLOTS + other] == codes[k * SLOTS + b]
                    total += a_ref[0, k, other].astype(F32) * jnp.where(same, 1.0, 0.0)
                merged[k, b] = total.astype(BF16)
            merged[k, SLOTS] = jnp.zeros((BLK, BLK), BF16)
            return None

        lax.fori_loop(0, TILES, merge, None)

        def place(zz, _):
            parity, from_y = maker(zz)
            for xl in (0, 1):
                q = NY * xl + from_y
                for cc in (0, 1):
                    k = 2 * parity + cc
                    for i in range(SLOTS):
                        slot = SLOTS
                        for b in range(SLOTS):
                            slot = jnp.where(codes[k * SLOTS + b] == i * SLOTS + q, b, slot)
                        dense[xl, zz, i * BLK:(i + 1) * BLK, cc * BLK:(cc + 1) * BLK] = merged[k, slot]
            return None

        lax.fori_loop(0, NZ, place, None)

    swap_own(0)
    slab_start()
    slab_own()
    lay_out_strip()
    for copy in inputs[3:]:
        copy.wait()
    selfpre[...] = jnp.dot(x_ref[...], ws_ref[...], preferred_element_type=F32) + bias_ref[...]
    gather(0, {})
    half_columns = [slice(h * HALF, (h + 1) * HALF) for h in (0, 1)]
    for h, columns in enumerate(half_columns):
        halfsend[h] = acc[:, columns].astype(BF16).reshape(REPS, BLK, HALF)
        for to in others:
            remote(halfsend.at[h, to], halfrecv.at[h, rep], rssend.at[0], halfsem.at[h], row, to).start()
    pre_halves = []
    for h, columns in enumerate(half_columns):
        total = acc[pl.ds(pl.multiple_of(rep * BLK, BLK), BLK), columns] + selfpre[:, columns]
        wait_for(halfrecv.at[h, pl.ds(0, REPS - 1)], halfsem.at[h])
        for other in others:
            total += halfrecv[h, other].astype(F32)
        sigma = jax.nn.sigmoid(total)
        slope = og_ref[:, columns].astype(F32) * sigma * (1.0 + total * (1.0 - sigma))
        own[1, h] = slope.astype(BF16)
        swap_own(1, (h,))
        act_ref[:, columns] = (total * sigma).astype(BF16)
    slab_other()
    pre_grad = jnp.concatenate([own[1, 0], own[1, 1]], axis=1)
    grad_start(0, lambda rows: jnp.dot(slab[rep, rows, :], pre_grad, preferred_element_type=F32))
    fg_self = lax.dot_general(pre_grad, ws_ref[...], (((1,), (1,)), ((), ())), preferred_element_type=F32)
    grad_to_layer(0)

    gather(1, {
        "stepped": lambda: grad_to_ring(0),
        "gathered": lambda: grad_from_ring(0),
    })
    round_partial(1)
    slab_end()

    def slab_product(rows):
        total = jnp.zeros((FIN // 2, FO), F32)
        for pair in range(REPS // 2):
            left = jnp.concatenate([slab[2 * pair, rows, :], slab[2 * pair + 1, rows, :]], axis=1)
            right = psend[1, 2 * pair:2 * pair + 2].reshape(2 * BLK, FO)
            total += jnp.dot(left, right, preferred_element_type=F32)
        return total

    grad_start(1, slab_product)
    grad_to_layer(1)
    total = jnp.zeros((8, FO), F32)
    ones = jnp.ones((8, 2 * BLK), BF16)
    for xl in (0, 1):
        for zz in range(NZ):
            both = jnp.concatenate([units[1, 0, xl, zz], units[1, 1, xl, zz]], axis=1)
            total += jnp.dot(ones, both, preferred_element_type=F32)
    bown[...] = total
    for to in others:
        remote(bown, brecv.at[rep], bsend, bread, row, to).start()
    grad_to_ring(1)
    scatter(1)
    grad_share(0)
    grad_from_ring(1)
    hidden = collect(1).astype(BF16)
    fg_ref[...] = (
        fg_self + lax.dot_general(hidden, wn_ref[...], (((1,), (1,)), ((), ())), preferred_element_type=F32)
    ).astype(BF16)
    wait_for(brecv.at[pl.ds(0, REPS - 1)], bread)
    brecv[rep] = bown[...]
    total = brecv[0, 0:1, :]
    for q in range(1, REPS):
        total += brecv[q, 0:1, :]
    bg_ref[...] = total
    grad_end(0)
    for which in (0, 1):
        for k in (0, 1):
            for h in (0, 1):
                @pl.when(elsewhere(goal(k, h), goal_rep))
                def _():
                    wait_for(own.at[which, h], asend.at[which, 2 * k + h])

        wait_for(units.at[which, 0, 0, pl.ds(0, 2)], xsend.at[which])
        wait_for(units.at[which, 0, 0, pl.ds(0, 6)], zsend.at[which])
        wait_for(units.at[which, 0, 0, pl.ds(0, 6)], dsend.at[which])
        wait_for(units.at[which, 0], csend.at[which])
        wait_for(psend.at[which, pl.ds(0, REPS - 1)], rssend.at[which])
    wait_for(brecv.at[pl.ds(0, REPS - 1)], bsend)
    wait_for(slab.at[pl.ds(0, REPS - 1)], slabsend)
    grad_drain(0)
    grad_share(1)
    grad_end(1)
    grad_drain(1)


def finish(act_in, fg_in, full, bias_in, act_ref, fg_ref, sg_ref, ng_ref, bg_ref):
    scale = NODES ** -0.5
    rows = FIN // PARTS
    for a, out_ref in enumerate((sg_ref, ng_ref)):
        for h in (0, 1):
            out_ref[:, h * HALF:(h + 1) * HALF] = full[a, h].reshape(rows, HALF).astype(F32) * scale
    act_ref[...] = act_in[...]
    fg_ref[...] = fg_in[...]
    bg_ref[...] = bias_in[...] * scale


def shards(node_features, self_weight, neigh_weight, bias, block_values, block_coords, block_counts, out_grad):
    vmem = pl.BlockSpec(memory_space=pltpu.VMEM)
    smem = pl.BlockSpec(memory_space=pltpu.SMEM)
    hbm = pl.BlockSpec(memory_space=pltpu.HBM)
    dma = pltpu.SemaphoreType.DMA
    outs = pl.pallas_call(
        kernel,
        out_shape=(
            jax.ShapeDtypeStruct((BLK, FO), BF16),
            jax.ShapeDtypeStruct((BLK, FIN), BF16),
            jax.ShapeDtypeStruct((2, 2, CHIPS, PIECE, HALF), BF16),
            jax.ShapeDtypeStruct((1, FO), F32),
        ),
        in_specs=[hbm, hbm, hbm, hbm, hbm, smem, smem, hbm],
        out_specs=(vmem,) * 4,
        scratch_shapes=[
            pltpu.VMEM((BLK, FIN), BF16),
            pltpu.VMEM((FIN, FO), BF16),
            pltpu.VMEM((FIN, FO), BF16),
            pltpu.VMEM((1, FO), F32),
            pltpu.VMEM((1, TILES, SLOTS, BLK, BLK), BF16),
            pltpu.VMEM((BLK, FO), BF16),
            dma((6,)),
            pltpu.SMEM((TILES * SLOTS,), jnp.int32),
            pltpu.VMEM((TILES, SLOTS + 1, BLK, BLK), BF16),
            pltpu.VMEM((2, NZ, SLOTS * BLK, 2 * BLK), BF16),
            pltpu.VMEM((2, 2, 2, NZ, 2 * BLK, HALF), BF16),
            pltpu.VMEM((2, 2, BLK, HALF), BF16),
            pltpu.VMEM((SLOTS * BLK, FO), F32),
            pltpu.VMEM((2, REPS, BLK, FO), BF16),
            pltpu.VMEM((2, REPS, BLK, FO), BF16),
            pltpu.VMEM((BLK, FO), F32),
            pltpu.VMEM((2, 2, FIN, HALF), BF16),
            pltpu.VMEM((2, FIN, HALF), BF16),
            pltpu.VMEM((2, CHIPS, PIECE, HALF), BF16),
            pltpu.VMEM((2, CHIPS, PIECE, HALF), BF16),
            pltpu.VMEM((2, NZ, PIECE, HALF), BF16),
            pltpu.VMEM((8, FO), F32),
            pltpu.VMEM((REPS, 8, FO), F32),
            pltpu.VMEM((REPS, FIN, BLK), BF16),
            pltpu.VMEM((2, REPS, BLK, HALF), BF16),
            pltpu.VMEM((2, REPS, BLK, HALF), BF16),
            dma((2,)),
            dma((2, 4)), dma((2, 2 * NZ)), dma((2, 2 * NZ)), dma((2, 4)),
            dma((2,)), dma((2,)), dma((2,)), dma((2,)), dma((2,)), dma((2,)),
            dma((2, 2)), dma((2, 2)), dma((2,)), dma((2,)), dma((2,)), dma((2,)),
            dma((2,)), dma((2,)), dma((2,)), dma((2,)),
            dma, dma, dma, dma((3,)),
        ],
        compiler_params=pltpu.CompilerParams(
            collective_id=0, has_side_effects=True, vmem_limit_bytes=56 * 1024 * 1024
        ),
        cost_estimate=pl.CostEstimate(flops=5 * 10 ** 9, bytes_accessed=6 * 10 ** 6, transcendentals=BLK * FO),
        name="sage_layer",
    )(
        node_features, self_weight, neigh_weight, bias.reshape(1, FO), block_values, block_coords.swapaxes(2, 3), block_counts,
        out_grad,
    )
    act, fg, sg, ng, bg = pl.pallas_call(
        finish,
        out_shape=(
            jax.ShapeDtypeStruct((BLK, FO), BF16),
            jax.ShapeDtypeStruct((BLK, FIN), BF16),
            jax.ShapeDtypeStruct((FIN, FO), F32),
            jax.ShapeDtypeStruct((FIN, FO), F32),
            jax.ShapeDtypeStruct((1, FO), F32),
        ),
        grid=(PARTS,),
        in_specs=[
            pl.BlockSpec((BLK // PARTS, FO), lambda i: (i, 0)),
            pl.BlockSpec((BLK // PARTS, FIN), lambda i: (i, 0)),
            pl.BlockSpec((2, 2, CHIPS // PARTS, PIECE, HALF), lambda i: (0, 0, i, 0, 0)),
            pl.BlockSpec((1, FO), lambda i: (0, 0)),
        ],
        out_specs=(
            pl.BlockSpec((BLK // PARTS, FO), lambda i: (i, 0)),
            pl.BlockSpec((BLK // PARTS, FIN), lambda i: (i, 0)),
            pl.BlockSpec((FIN // PARTS, FO), lambda i: (i, 0)),
            pl.BlockSpec((FIN // PARTS, FO), lambda i: (i, 0)),
            pl.BlockSpec((1, FO), lambda i: (0, 0)),
        ),
        compiler_params=pltpu.CompilerParams(vmem_limit_bytes=56 * 1024 * 1024),
        name="finish",
    )(*outs)
    return act, fg, sg, ng, bg.reshape(FO)


def solution(mesh):
    nodes = P(("row", "rep"), None)
    placed = (
        nodes, P(), P(), P(), P("row", "rep", None, None, None), P("row", "rep", None, None), P("row", "rep"), nodes,
    )
    return jax.shard_map(
        shards, mesh=mesh, in_specs=placed, out_specs=(nodes, nodes, P(), P(), P()), check_vma=False
    )
```

```python
import jax
import jax.numpy as jnp
from jax import lax
from jax.experimental import pallas as pl
from jax.experimental.pallas import tpu as pltpu
from jax.sharding import PartitionSpec as P

MESH = pl.DeviceIdType.MESH
BF16 = jnp.bfloat16
F32 = jnp.float32
FIN, FO, BLK, SLOTS, TILES = 768, 256, 128, 8, 4
ROWS, REPS, NY, NZ, CHIPS = 32, 8, 4, 8, 16
HALF = FO // 2
PIECE = FIN // CHIPS
PARTS = 2
NODES = ROWS * REPS * BLK
Z_STEP = ((0, 1), (0, -1), (1, 1), (1, -1), (0, 2), (0, -2))


def wait_for(ref, sem):
    pltpu.make_async_copy(ref, ref, sem).wait()


def kernel(
    x_hbm, ws_hbm, wn_hbm, bias_hbm, a_hbm, coords_ref, counts_ref, og_hbm,
    act_ref, fg_ref, full, bg_ref,
    x_ref, ws_ref, wn_ref, bias_ref, a_ref, og_ref, insem,
    codes, merged, dense, units, own, acc, psend, precv, selfpre,
    halves, sibrecv, pieces, piecerecv, ringrecv, bown, brecv, slab,
    halfsend, halfrecv, halfsem,
    arecv, urecv, crecv, asend, xsend, zsend, dsend, csend, rssend, rsrecv,
    s1send, s1recv, p1send, p1recv, r1send, r1recv, q1send, q1recv, s2send, s2recv, bsend, bread,
    slabsend, slabrecv,
):
    row = lax.axis_index("row")
    rep = lax.axis_index("rep")
    core = lax.rem(row, 2)
    chip = lax.div(row, 2)
    z = lax.rem(chip, NZ)
    xlo = lax.div(chip, NZ)
    xhi = lax.div(rep, NY)
    y = lax.rem(rep, NY)

    def row_at(xl, zz, cc):
        return (xl * NZ + zz) * 2 + cc

    def around(zz):
        return lax.rem(zz + 2 * NZ, NZ)

    across = row_at(1 - xlo, z, core)
    sibling = row_at(xlo, z, 1 - core)

    goal_y, odd = lax.div(z, 2), lax.rem(z, 2)
    home = around(2 * goal_y + NY * odd + lax.rem(odd + y - goal_y + NY, NY))
    goal_rep = xlo * NY + goal_y

    def goal(k, h):
        return row_at(xhi, around(home + 4 * k), h)

    def maker(zz):
        place = around(zz - 2 * y)
        parity = lax.div(place, NY)
        return parity, lax.rem(lax.rem(place, NY) - parity + y + NY, NY)

    def origin(k, cc):
        parity, from_y = maker(around(z + 4 * k))
        return row_at(xhi, 2 * y + parity, cc), xlo * NY + from_y

    def elsewhere(to_row, to_rep):
        return jnp.logical_or(to_row != row, to_rep != rep)

    inputs = [
        pltpu.make_async_copy(src, dst, insem.at[i])
        for i, (src, dst) in enumerate((
            (x_hbm, x_ref), (wn_hbm, wn_ref), (a_hbm, a_ref), (ws_hbm, ws_ref), (og_hbm, og_ref), (bias_hbm, bias_ref),
        ))
    ]
    for copy in inputs:
        copy.start()

    barrier = pltpu.get_barrier_semaphore()

    def greet(to_row, to_rep):
        pl.semaphore_signal(barrier, inc=1, device_id=(to_row, to_rep), device_id_type=MESH)

    goals = 0
    for k in (0, 1):
        for h in (0, 1):
            from_row, from_rep = origin(k, h)

            @pl.when(elsewhere(from_row, from_rep))
            def _():
                greet(from_row, from_rep)

            goals += jnp.where(elsewhere(goal(k, h), goal_rep), 1, 0)
    lax.fori_loop(1, REPS, lambda d, _: greet(row, lax.rem(rep + d, REPS)), None)
    lax.fori_loop(0, REPS, lambda to, _: greet(row_at(1 - xlo, z, core), to), None)
    lax.fori_loop(1, NZ, lambda d, _: greet(row_at(xlo, around(z + d), core), rep), None)
    greet(sibling, rep)

    for copy in inputs[:2]:
        copy.wait()

    def keep(which, value):
        own[which, 0] = value[:, :HALF]
        own[which, 1] = value[:, HALF:]

    keep(0, jnp.dot(x_ref[...], wn_ref[...], preferred_element_type=F32).astype(BF16))

    pl.semaphore_wait(barrier, REPS - 1 + REPS + NZ - 1 + 1 + goals)

    def remote(src, dst, ssem, rsem, to_row, to_rep):
        return pltpu.make_async_remote_copy(
            src_ref=src, dst_ref=dst, send_sem=ssem, recv_sem=rsem,
            device_id=(to_row, to_rep), device_id_type=MESH,
        )

    def swap_own(which, columns=(0, 1)):
        place = pl.ds(pl.multiple_of(core * BLK, BLK), BLK)
        for h in columns:
            for k in (0, 1):
                far = elsewhere(goal(k, h), goal_rep)

                @pl.when(far)
                def _():
                    remote(
                        own.at[which, h], units.at[which, h, xhi, home, place, :],
                        asend.at[which, 2 * k + h], arecv.at[which, 2 * k + core], goal(k, h), goal_rep,
                    ).start()

                @pl.when(jnp.logical_not(far))
                def _():
                    units[which, h, xhi, home, place, :] = own[which, h]

    others = [
        lax.rem(xhi + dx, 2) * NY + lax.rem(y + dy, NY)
        for dx, dy in ((1, 2), (1, 1), (1, 3), (0, 2), (1, 0), (0, 1), (0, 3))
    ]

    layer = [
        (lax.rem(xlo + dxlo, 2), lax.rem(xhi + dxhi, 2) * NY + lax.rem(y + dy, NY))
        for dxhi, dxlo, dy in (
            (1, 0, 2), (1, 0, 1), (1, 0, 3), (1, 0, 0), (0, 0, 2), (0, 0, 1), (0, 0, 3),
            (1, 1, 2), (0, 1, 2), (1, 1, 1), (1, 1, 3), (0, 1, 1), (0, 1, 3), (1, 1, 0), (0, 1, 0),
        )
    ]
    mine = xlo * REPS + rep

    def column(peer):
        return 1 - xlo if peer else xlo

    def gather(which, hooks):
        def unit(peer, offset, h):
            return units.at[which, h, column(peer), around(z + offset)]

        def arrival(peer, offset):
            return urecv.at[which, 8 * peer + offset % NZ]

        def share(peer, offset):
            piece = unit(peer, offset, core)
            remote(piece, piece, csend.at[which], crecv.at[which, 8 * peer + offset % NZ], sibling, rep).start()

        def step_z(peer, sem):
            for held, distance in Z_STEP:
                piece = unit(peer, 4 * held, core)
                to = row_at(xlo, around(z + distance), core)
                remote(piece, piece, sem, arrival(peer, 4 * held - distance), to, rep).start()

        def step_x(offset, sem):
            piece = unit(0, offset, core)
            remote(piece, piece, sem, arrival(1, offset), across, rep).start()

        first = [True]

        def add_unit(peer, offset):
            wait_for(unit(peer, offset, core), crecv.at[which, 8 * peer + offset % NZ])
            both = jnp.concatenate([unit(peer, offset, 0)[...], unit(peer, offset, 1)[...]], axis=1)
            part = jnp.dot(dense[column(peer), around(z + offset)], both, preferred_element_type=F32)
            if first[0]:
                acc[...] = part
            else:
                acc[...] += part
            first[0] = False

        def hook(name):
            hooks.get(name, lambda: None)()

        for k in (0, 1):
            for cc in (0, 1):
                @pl.when(elsewhere(*origin(k, cc)))
                def _():
                    wait_for(own.at[which, 0], arecv.at[which, 2 * k + cc])
        step_x(0, xsend.at[which])
        step_x(4, xsend.at[which])
        step_z(0, zsend.at[which])
        share(0, 0)
        share(0, 4)
        hook("swapped")
        for offset in (0, 4):
            wait_for(unit(1, offset, core), arrival(1, offset))

        @pl.when(core == 0)
        def _():
            step_z(1, dsend.at[which])

        share(1, 0)
        share(1, 4)
        offsets = [4 * held - distance for held, distance in Z_STEP]
        for offset in offsets:
            wait_for(unit(0, offset, core), arrival(0, offset))

            @pl.when(core == 1)
            def _():
                step_x(offset, dsend.at[which])

            share(0, offset)
        hook("stepped")
        rest = [(0, 0), (0, 4), (1, 0), (1, 4)] + [(0, offset) for offset in offsets]
        for i, offset in enumerate(offsets):
            for peer, earlier in rest[2 * i:2 * i + 2]:
                add_unit(peer, earlier)
            if i >= 2:
                add_unit(1, offsets[i - 2])
            wait_for(unit(1, offset, core), arrival(1, offset))
            share(1, offset)
        hook("gathered")
        for offset in offsets[-2:]:
            add_unit(1, offset)

    def round_partial(which):
        psend[which] = acc[...].astype(BF16).reshape(REPS, BLK, FO)

    def scatter(which):
        for to in others:
            remote(
                psend.at[which, to], precv.at[which, rep], rssend.at[which], rsrecv.at[which], row, to
            ).start()

    def collect(which):
        total = acc[pl.ds(pl.multiple_of(rep * BLK, BLK), BLK), :]
        wait_for(precv.at[which, pl.ds(0, REPS - 1)], rsrecv.at[which])
        for other in others:
            total += precv[which, other].astype(F32)
        return total

    opposite = lax.rem(xhi + 1, 2) * NY + y
    beside = [xhi * NY + lax.rem(y + dy, NY) for dy in (2, 1, 3)]

    def slab_start():
        slab[rep] = x_ref[...].T
        remote(slab.at[rep], slab.at[rep], slabsend, slabrecv.at[0], row, opposite).start()

    def slab_own():
        for to in beside:
            remote(slab.at[rep], slab.at[rep], slabsend, slabrecv.at[1], row, to).start()

    def slab_other():
        wait_for(slab.at[opposite], slabrecv.at[0])
        for to in beside:
            remote(slab.at[opposite], slab.at[opposite], slabsend, slabrecv.at[2], row, to).start()

    def slab_end():
        wait_for(slab.at[pl.ds(0, NY - 1)], slabrecv.at[1])
        wait_for(slab.at[pl.ds(0, NY - 1)], slabrecv.at[2])

    def rows_for(d):
        return pl.ds(pl.multiple_of(lax.rem(xlo + d, 2) * (FIN // 2), FIN // 2), FIN // 2)

    def grad_start(a, product):
        for d in (0, 1):
            rows = rows_for(d)
            part = product(rows)
            halves[a, 0, rows, :] = part[:, :HALF].astype(BF16)
            halves[a, 1, rows, :] = part[:, HALF:].astype(BF16)
            remote(
                halves.at[a, 1 - core, rows], sibrecv.at[a, rows], s1send.at[a, d], s1recv.at[a, d], sibling, rep
            ).start()

    def grad_to_layer(a):
        for d in (0, 1):
            rows = rows_for(d)
            wait_for(sibrecv.at[a, rows], s1recv.at[a, d])
            both = halves[a, core, rows, :].astype(F32) + sibrecv[a, rows, :].astype(F32)
            owned = pl.ds(pl.multiple_of(lax.rem(xlo + d, 2) * REPS, REPS), REPS)
            pieces[a, owned] = both.astype(BF16).reshape(REPS, PIECE, HALF)
            for xl, to in layer[:7] if d == 0 else layer[7:]:
                remote(
                    pieces.at[a, xl * REPS + to], piecerecv.at[a, mine], p1send.at[a], p1recv.at[a],
                    row_at(xl, z, core), to,
                ).start()

    def grad_to_ring(a):
        total = pieces[a, mine].astype(F32)
        wait_for(piecerecv.at[a, pl.ds(0, CHIPS - 1)], p1recv.at[a])
        for xl, other in layer:
            total += piecerecv[a, xl * REPS + other].astype(F32)
        ringrecv[a, z] = total.astype(BF16)
        for d in (4, 3, 5, 2, 6, 1, 7):
            place = ringrecv.at[a, z]
            to = row_at(xlo, around(z + d), core)
            remote(place, place, r1send.at[a], r1recv.at[a], to, rep).start()

    def grad_from_ring(a):
        wait_for(ringrecv.at[a, pl.ds(0, NZ - 1)], r1recv.at[a])
        total = ringrecv[a, 0].astype(F32)
        for zz in range(1, NZ):
            total += ringrecv[a, zz].astype(F32)
        full[a, core, mine] = total.astype(BF16)
        piece = full.at[a, core, mine]
        for d in (0, 1):
            for xl, to in layer[:7] if d == 0 else layer[7:]:
                remote(piece, piece, q1send.at[a], q1recv.at[a, d], row_at(xl, z, core), to).start()

    def grad_share(a):
        for d in (0, 1):
            wait_for(full.at[a, core, pl.ds(0, REPS - 1 + d)], q1recv.at[a, d])
            owned = pl.ds(pl.multiple_of(lax.rem(xlo + d, 2) * REPS, REPS), REPS)
            part = full.at[a, core, owned]
            remote(part, part, s2send.at[a], s2recv.at[a], sibling, rep).start()

    def grad_end(a):
        wait_for(full.at[a, 1 - core], s2recv.at[a])

    def grad_drain(a):
        for d in (0, 1):
            wait_for(sibrecv.at[a, rows_for(d)], s1send.at[a, d])
        wait_for(piecerecv.at[a, pl.ds(0, CHIPS - 1)], p1send.at[a])
        wait_for(ringrecv.at[a, pl.ds(0, NZ - 1)], r1send.at[a])
        wait_for(full.at[a, core, pl.ds(0, CHIPS - 1)], q1send.at[a])
        wait_for(full.at[a, core], s2send.at[a])

    def lay_out_strip():
        inputs[2].wait()

        def merge(k, _):
            for b in range(SLOTS):
                where = coords_ref[0, k, 0, b] * SLOTS + coords_ref[0, k, 1, b]
                codes[k * SLOTS + b] = jnp.where(b < counts_ref[0, k], where, 255)
            for b in range(SLOTS):
                total = a_ref[0, k, b].astype(F32)
                for other in range(b):
                    same = codes[k * SLOTS + other] == codes[k * SLOTS + b]
                    total += a_ref[0, k, other].astype(F32) * jnp.where(same, 1.0, 0.0)
                merged[k, b] = total.astype(BF16)
            merged[k, SLOTS] = jnp.zeros((BLK, BLK), BF16)
            return None

        lax.fori_loop(0, TILES, merge, None)

        def place(zz, _):
            parity, from_y = maker(zz)
            for xl in (0, 1):
                q = NY * xl + from_y
                for cc in (0, 1):
                    k = 2 * parity + cc
                    for i in range(SLOTS):
                        slot = SLOTS
                        for b in range(SLOTS):
                            slot = jnp.where(codes[k * SLOTS + b] == i * SLOTS + q, b, slot)
                        dense[xl, zz, i * BLK:(i + 1) * BLK, cc * BLK:(cc + 1) * BLK] = merged[k, slot]
            return None

        lax.fori_loop(0, NZ, place, None)

    swap_own(0)
    slab_start()
    slab_own()
    lay_out_strip()
    for copy in inputs[3:]:
        copy.wait()
    selfpre[...] = jnp.dot(x_ref[...], ws_ref[...], preferred_element_type=F32) + bias_ref[...]
    gather(0, {})
    half_columns = [slice(h * HALF, (h + 1) * HALF) for h in (0, 1)]
    for h, columns in enumerate(half_columns):
        halfsend[h] = acc[:, columns].astype(BF16).reshape(REPS, BLK, HALF)
        for to in others:
            remote(halfsend.at[h, to], halfrecv.at[h, rep], rssend.at[0], halfsem.at[h], row, to).start()
    pre_halves = []
    for h, columns in enumerate(half_columns):
        total = acc[pl.ds(pl.multiple_of(rep * BLK, BLK), BLK), columns] + selfpre[:, columns]
        wait_for(halfrecv.at[h, pl.ds(0, REPS - 1)], halfsem.at[h])
        for other in others:
            total += halfrecv[h, other].astype(F32)
        sigma = jax.nn.sigmoid(total)
        slope = og_ref[:, columns].astype(F32) * sigma * (1.0 + total * (1.0 - sigma))
        own[1, h] = slope.astype(BF16)
        swap_own(1, (h,))
        act_ref[:, columns] = (total * sigma).astype(BF16)
    slab_other()
    pre_grad = jnp.concatenate([own[1, 0], own[1, 1]], axis=1)
    grad_start(0, lambda rows: jnp.dot(slab[rep, rows, :], pre_grad, preferred_element_type=F32))
    fg_self = lax.dot_general(pre_grad, ws_ref[...], (((1,), (1,)), ((), ())), preferred_element_type=F32)
    grad_to_layer(0)

    gather(1, {
        "stepped": lambda: grad_to_ring(0),
        "gathered": lambda: grad_from_ring(0),
    })
    round_partial(1)
    slab_end()

    def slab_product(rows):
        total = jnp.zeros((FIN // 2, FO), F32)
        for pair in range(REPS // 2):
            left = jnp.concatenate([slab[2 * pair, rows, :], slab[2 * pair + 1, rows, :]], axis=1)
            right = psend[1, 2 * pair:2 * pair + 2].reshape(2 * BLK, FO)
            total += jnp.dot(left, right, preferred_element_type=F32)
        return total

    grad_start(1, slab_product)
    grad_to_layer(1)
    total = jnp.zeros((8, FO), F32)
    ones = jnp.ones((8, 2 * BLK), BF16)
    for xl in (0, 1):
        for zz in range(NZ):
            both = jnp.concatenate([units[1, 0, xl, zz], units[1, 1, xl, zz]], axis=1)
            total += jnp.dot(ones, both, preferred_element_type=F32)
    bown[...] = total
    for to in others:
        remote(bown, brecv.at[rep], bsend, bread, row, to).start()
    grad_to_ring(1)
    scatter(1)
    grad_share(0)
    grad_from_ring(1)
    hidden = collect(1).astype(BF16)
    fg_ref[...] = (
        fg_self + lax.dot_general(hidden, wn_ref[...], (((1,), (1,)), ((), ())), preferred_element_type=F32)
    ).astype(BF16)
    wait_for(brecv.at[pl.ds(0, REPS - 1)], bread)
    brecv[rep] = bown[...]
    total = brecv[0, 0:1, :]
    for q in range(1, REPS):
        total += brecv[q, 0:1, :]
    bg_ref[...] = total
    grad_end(0)
    for which in (0, 1):
        for k in (0, 1):
            for h in (0, 1):
                @pl.when(elsewhere(goal(k, h), goal_rep))
                def _():
                    wait_for(own.at[which, h], asend.at[which, 2 * k + h])

        wait_for(units.at[which, 0, 0, pl.ds(0, 2)], xsend.at[which])
        wait_for(units.at[which, 0, 0, pl.ds(0, 6)], zsend.at[which])
        wait_for(units.at[which, 0, 0, pl.ds(0, 6)], dsend.at[which])
        wait_for(units.at[which, 0], csend.at[which])
        wait_for(psend.at[which, pl.ds(0, REPS - 1)], rssend.at[which])
    wait_for(brecv.at[pl.ds(0, REPS - 1)], bsend)
    wait_for(slab.at[pl.ds(0, REPS - 1)], slabsend)
    grad_drain(0)
    grad_share(1)
    grad_end(1)
    grad_drain(1)


def finish(act_in, fg_in, full, bias_in, act_ref, fg_ref, sg_ref, ng_ref, bg_ref):
    scale = NODES ** -0.5
    rows = FIN // PARTS
    for a, out_ref in enumerate((sg_ref, ng_ref)):
        for h in (0, 1):
            out_ref[:, h * HALF:(h + 1) * HALF] = full[a, h].reshape(rows, HALF).astype(F32) * scale
    act_ref[...] = act_in[...]
    fg_ref[...] = fg_in[...]
    bg_ref[...] = bias_in[...] * scale


def shards(node_features, self_weight, neigh_weight, bias, block_values, block_coords, block_counts, out_grad):
    vmem = pl.BlockSpec(memory_space=pltpu.VMEM)
    smem = pl.BlockSpec(memory_space=pltpu.SMEM)
    hbm = pl.BlockSpec(memory_space=pltpu.HBM)
    dma = pltpu.SemaphoreType.DMA
    outs = pl.pallas_call(
        kernel,
        out_shape=(
            jax.ShapeDtypeStruct((BLK, FO), BF16),
            jax.ShapeDtypeStruct((BLK, FIN), BF16),
            jax.ShapeDtypeStruct((2, 2, CHIPS, PIECE, HALF), BF16),
            jax.ShapeDtypeStruct((1, FO), F32),
        ),
        in_specs=[hbm, hbm, hbm, hbm, hbm, smem, smem, hbm],
        out_specs=(vmem,) * 4,
        scratch_shapes=[
            pltpu.VMEM((BLK, FIN), BF16),
            pltpu.VMEM((FIN, FO), BF16),
            pltpu.VMEM((FIN, FO), BF16),
            pltpu.VMEM((1, FO), F32),
            pltpu.VMEM((1, TILES, SLOTS, BLK, BLK), BF16),
            pltpu.VMEM((BLK, FO), BF16),
            dma((6,)),
            pltpu.SMEM((TILES * SLOTS,), jnp.int32),
            pltpu.VMEM((TILES, SLOTS + 1, BLK, BLK), BF16),
            pltpu.VMEM((2, NZ, SLOTS * BLK, 2 * BLK), BF16),
            pltpu.VMEM((2, 2, 2, NZ, 2 * BLK, HALF), BF16),
            pltpu.VMEM((2, 2, BLK, HALF), BF16),
            pltpu.VMEM((SLOTS * BLK, FO), F32),
            pltpu.VMEM((2, REPS, BLK, FO), BF16),
            pltpu.VMEM((2, REPS, BLK, FO), BF16),
            pltpu.VMEM((BLK, FO), F32),
            pltpu.VMEM((2, 2, FIN, HALF), BF16),
            pltpu.VMEM((2, FIN, HALF), BF16),
            pltpu.VMEM((2, CHIPS, PIECE, HALF), BF16),
            pltpu.VMEM((2, CHIPS, PIECE, HALF), BF16),
            pltpu.VMEM((2, NZ, PIECE, HALF), BF16),
            pltpu.VMEM((8, FO), F32),
            pltpu.VMEM((REPS, 8, FO), F32),
            pltpu.VMEM((REPS, FIN, BLK), BF16),
            pltpu.VMEM((2, REPS, BLK, HALF), BF16),
            pltpu.VMEM((2, REPS, BLK, HALF), BF16),
            dma((2,)),
            dma((2, 4)), dma((2, 2 * NZ)), dma((2, 2 * NZ)), dma((2, 4)),
            dma((2,)), dma((2,)), dma((2,)), dma((2,)), dma((2,)), dma((2,)),
            dma((2, 2)), dma((2, 2)), dma((2,)), dma((2,)), dma((2,)), dma((2,)),
            dma((2,)), dma((2, 2)), dma((2,)), dma((2,)),
            dma, dma, dma, dma((3,)),
        ],
        compiler_params=pltpu.CompilerParams(
            collective_id=0, has_side_effects=True, vmem_limit_bytes=56 * 1024 * 1024
        ),
        cost_estimate=pl.CostEstimate(flops=5 * 10 ** 9, bytes_accessed=6 * 10 ** 6, transcendentals=BLK * FO),
        name="sage_layer",
    )(
        node_features, self_weight, neigh_weight, bias.reshape(1, FO), block_values, block_coords.swapaxes(2, 3), block_counts,
        out_grad,
    )
    act, fg, sg, ng, bg = pl.pallas_call(
        finish,
        out_shape=(
            jax.ShapeDtypeStruct((BLK, FO), BF16),
            jax.ShapeDtypeStruct((BLK, FIN), BF16),
            jax.ShapeDtypeStruct((FIN, FO), F32),
            jax.ShapeDtypeStruct((FIN, FO), F32),
            jax.ShapeDtypeStruct((1, FO), F32),
        ),
        grid=(PARTS,),
        in_specs=[
            pl.BlockSpec((BLK // PARTS, FO), lambda i: (i, 0)),
            pl.BlockSpec((BLK // PARTS, FIN), lambda i: (i, 0)),
            pl.BlockSpec((2, 2, CHIPS // PARTS, PIECE, HALF), lambda i: (0, 0, i, 0, 0)),
            pl.BlockSpec((1, FO), lambda i: (0, 0)),
        ],
        out_specs=(
            pl.BlockSpec((BLK // PARTS, FO), lambda i: (i, 0)),
            pl.BlockSpec((BLK // PARTS, FIN), lambda i: (i, 0)),
            pl.BlockSpec((FIN // PARTS, FO), lambda i: (i, 0)),
            pl.BlockSpec((FIN // PARTS, FO), lambda i: (i, 0)),
            pl.BlockSpec((1, FO), lambda i: (0, 0)),
        ),
        compiler_params=pltpu.CompilerParams(vmem_limit_bytes=56 * 1024 * 1024),
        name="finish",
    )(*outs)
    return act, fg, sg, ng, bg.reshape(FO)


def solution(mesh):
    nodes = P(("row", "rep"), None)
    placed = (
        nodes, P(), P(), P(), P("row", "rep", None, None, None), P("row", "rep", None, None), P("row", "rep"), nodes,
    )
    return jax.shard_map(
        shards, mesh=mesh, in_specs=placed, out_specs=(nodes, nodes, P(), P(), P()), check_vma=False
    )
```

```python
import jax
import jax.numpy as jnp
from jax import lax
from jax.experimental import pallas as pl
from jax.experimental.pallas import tpu as pltpu
from jax.sharding import PartitionSpec as P

MESH = pl.DeviceIdType.MESH
BF16 = jnp.bfloat16
F32 = jnp.float32
FIN, FO, BLK, SLOTS, TILES = 768, 256, 128, 8, 4
ROWS, REPS, NY, NZ, CHIPS = 32, 8, 4, 8, 16
HALF = FO // 2
PIECE = FIN // CHIPS
PARTS = 2
NODES = ROWS * REPS * BLK
Z_STEP = ((0, 1), (0, -1), (1, 1), (1, -1), (0, 2), (0, -2))


def wait_for(ref, sem):
    pltpu.make_async_copy(ref, ref, sem).wait()


def kernel(
    x_hbm, ws_hbm, wn_hbm, bias_hbm, a_hbm, coords_ref, counts_ref, og_hbm,
    act_ref, fg_ref, full, bg_ref,
    x_ref, ws_ref, wn_ref, bias_ref, a_ref, og_ref, insem,
    codes, merged, dense, units, own, acc, psend, precv, selfpre,
    halves, sibrecv, pieces, piecerecv, ringrecv, bown, brecv, slab,
    halfsend, halfrecv, halfsem,
    arecv, urecv, crecv, asend, xsend, zsend, dsend, csend, rssend, rsrecv,
    s1send, s1recv, p1send, p1recv, r1send, r1recv, q1send, q1recv, s2send, s2recv, bsend, bread,
    slabsend, slabrecv,
):
    row = lax.axis_index("row")
    rep = lax.axis_index("rep")
    core = lax.rem(row, 2)
    chip = lax.div(row, 2)
    z = lax.rem(chip, NZ)
    xlo = lax.div(chip, NZ)
    xhi = lax.div(rep, NY)
    y = lax.rem(rep, NY)

    def row_at(xl, zz, cc):
        return (xl * NZ + zz) * 2 + cc

    def around(zz):
        return lax.rem(zz + 2 * NZ, NZ)

    across = row_at(1 - xlo, z, core)
    sibling = row_at(xlo, z, 1 - core)

    goal_y, odd = lax.div(z, 2), lax.rem(z, 2)
    home = around(2 * goal_y + NY * odd + lax.rem(odd + y - goal_y + NY, NY))
    goal_rep = xlo * NY + goal_y

    def goal(k, h):
        return row_at(xhi, around(home + 4 * k), h)

    def maker(zz):
        place = around(zz - 2 * y)
        parity = lax.div(place, NY)
        return parity, lax.rem(lax.rem(place, NY) - parity + y + NY, NY)

    def origin(k, cc):
        parity, from_y = maker(around(z + 4 * k))
        return row_at(xhi, 2 * y + parity, cc), xlo * NY + from_y

    def elsewhere(to_row, to_rep):
        return jnp.logical_or(to_row != row, to_rep != rep)

    inputs = [
        pltpu.make_async_copy(src, dst, insem.at[i])
        for i, (src, dst) in enumerate((
            (x_hbm, x_ref), (wn_hbm, wn_ref), (a_hbm, a_ref), (ws_hbm, ws_ref), (og_hbm, og_ref), (bias_hbm, bias_ref),
        ))
    ]
    for copy in inputs:
        copy.start()

    barrier = pltpu.get_barrier_semaphore()

    def greet(to_row, to_rep):
        pl.semaphore_signal(barrier, inc=1, device_id=(to_row, to_rep), device_id_type=MESH)

    goals = 0
    for k in (0, 1):
        for h in (0, 1):
            from_row, from_rep = origin(k, h)

            @pl.when(elsewhere(from_row, from_rep))
            def _():
                greet(from_row, from_rep)

            goals += jnp.where(elsewhere(goal(k, h), goal_rep), 1, 0)
    lax.fori_loop(1, REPS, lambda d, _: greet(row, lax.rem(rep + d, REPS)), None)
    lax.fori_loop(0, REPS, lambda to, _: greet(row_at(1 - xlo, z, core), to), None)
    lax.fori_loop(1, NZ, lambda d, _: greet(row_at(xlo, around(z + d), core), rep), None)
    greet(sibling, rep)

    for copy in inputs[:2]:
        copy.wait()

    def keep(which, value):
        own[which, 0] = value[:, :HALF]
        own[which, 1] = value[:, HALF:]

    keep(0, jnp.dot(x_ref[...], wn_ref[...], preferred_element_type=F32).astype(BF16))

    pl.semaphore_wait(barrier, REPS - 1 + REPS + NZ - 1 + 1 + goals)

    def remote(src, dst, ssem, rsem, to_row, to_rep):
        return pltpu.make_async_remote_copy(
            src_ref=src, dst_ref=dst, send_sem=ssem, recv_sem=rsem,
            device_id=(to_row, to_rep), device_id_type=MESH,
        )

    def swap_own(which, columns=(0, 1)):
        place = pl.ds(pl.multiple_of(core * BLK, BLK), BLK)
        for h in columns:
            for k in (0, 1):
                far = elsewhere(goal(k, h), goal_rep)

                @pl.when(far)
                def _():
                    remote(
                        own.at[which, h], units.at[which, h, xhi, home, place, :],
                        asend.at[which, 2 * k + h], arecv.at[which, 2 * k + core], goal(k, h), goal_rep,
                    ).start()

                @pl.when(jnp.logical_not(far))
                def _():
                    units[which, h, xhi, home, place, :] = own[which, h]

    others = [
        lax.rem(xhi + dx, 2) * NY + lax.rem(y + dy, NY)
        for dx, dy in ((1, 2), (1, 1), (1, 3), (0, 2), (1, 0), (0, 1), (0, 3))
    ]

    layer = [
        (lax.rem(xlo + dxlo, 2), lax.rem(xhi + dxhi, 2) * NY + lax.rem(y + dy, NY))
        for dxhi, dxlo, dy in (
            (1, 0, 2), (1, 0, 1), (1, 0, 3), (1, 0, 0), (0, 0, 2), (0, 0, 1), (0, 0, 3),
            (1, 1, 2), (0, 1, 2), (1, 1, 1), (1, 1, 3), (0, 1, 1), (0, 1, 3), (1, 1, 0), (0, 1, 0),
        )
    ]
    mine = xlo * REPS + rep

    def column(peer):
        return 1 - xlo if peer else xlo

    def gather(which, hooks):
        def unit(peer, offset, h):
            return units.at[which, h, column(peer), around(z + offset)]

        def arrival(peer, offset):
            return urecv.at[which, 8 * peer + offset % NZ]

        def share(peer, offset):
            piece = unit(peer, offset, core)
            remote(piece, piece, csend.at[which], crecv.at[which, 8 * peer + offset % NZ], sibling, rep).start()

        def step_z(peer, sem):
            for held, distance in Z_STEP:
                piece = unit(peer, 4 * held, core)
                to = row_at(xlo, around(z + distance), core)
                remote(piece, piece, sem, arrival(peer, 4 * held - distance), to, rep).start()

        def step_x(offset, sem):
            piece = unit(0, offset, core)
            remote(piece, piece, sem, arrival(1, offset), across, rep).start()

        first = [True]

        def add_unit(peer, offset):
            wait_for(unit(peer, offset, core), crecv.at[which, 8 * peer + offset % NZ])
            both = jnp.concatenate([unit(peer, offset, 0)[...], unit(peer, offset, 1)[...]], axis=1)
            part = jnp.dot(dense[column(peer), around(z + offset)], both, preferred_element_type=F32)
            if first[0]:
                acc[...] = part
            else:
                acc[...] += part
            first[0] = False

        def hook(name):
            hooks.get(name, lambda: None)()

        for k in (0, 1):
            for cc in (0, 1):
                @pl.when(elsewhere(*origin(k, cc)))
                def _():
                    wait_for(own.at[which, 0], arecv.at[which, 2 * k + cc])
        step_x(0, xsend.at[which])
        step_x(4, xsend.at[which])
        step_z(0, zsend.at[which])
        share(0, 0)
        share(0, 4)
        hook("swapped")
        for offset in (0, 4):
            wait_for(unit(1, offset, core), arrival(1, offset))

        @pl.when(core == 0)
        def _():
            step_z(1, dsend.at[which])

        share(1, 0)
        share(1, 4)
        offsets = [4 * held - distance for held, distance in Z_STEP]
        for offset in offsets:
            wait_for(unit(0, offset, core), arrival(0, offset))

            @pl.when(core == 1)
            def _():
                step_x(offset, dsend.at[which])

            share(0, offset)
        hook("stepped")
        rest = [(0, 0), (0, 4), (1, 0), (1, 4)] + [(0, offset) for offset in offsets]
        for i, offset in enumerate(offsets):
            for peer, earlier in rest[2 * i:2 * i + 2]:
                add_unit(peer, earlier)
            if i >= 2:
                add_unit(1, offsets[i - 2])
            wait_for(unit(1, offset, core), arrival(1, offset))
            share(1, offset)
        hook("gathered")
        for offset in offsets[-2:]:
            add_unit(1, offset)

    def round_partial(which):
        psend[which] = acc[...].astype(BF16).reshape(REPS, BLK, FO)

    def scatter(which):
        for to in others:
            remote(
                psend.at[which, to], precv.at[which, rep], rssend.at[which], rsrecv.at[which], row, to
            ).start()

    def collect(which):
        total = acc[pl.ds(pl.multiple_of(rep * BLK, BLK), BLK), :]
        wait_for(precv.at[which, pl.ds(0, REPS - 1)], rsrecv.at[which])
        for other in others:
            total += precv[which, other].astype(F32)
        return total

    opposite = lax.rem(xhi + 1, 2) * NY + y
    beside = [xhi * NY + lax.rem(y + dy, NY) for dy in (2, 1, 3)]

    def slab_start():
        slab[rep] = x_ref[...].T
        remote(slab.at[rep], slab.at[rep], slabsend, slabrecv.at[0], row, opposite).start()

    def slab_own():
        for to in beside:
            remote(slab.at[rep], slab.at[rep], slabsend, slabrecv.at[1], row, to).start()

    def slab_other():
        wait_for(slab.at[opposite], slabrecv.at[0])
        for to in beside:
            remote(slab.at[opposite], slab.at[opposite], slabsend, slabrecv.at[2], row, to).start()

    def slab_end():
        wait_for(slab.at[pl.ds(0, NY - 1)], slabrecv.at[1])
        wait_for(slab.at[pl.ds(0, NY - 1)], slabrecv.at[2])

    def rows_for(d):
        return pl.ds(pl.multiple_of(lax.rem(xlo + d, 2) * (FIN // 2), FIN // 2), FIN // 2)

    def grad_start(a, product):
        for d in (0, 1):
            rows = rows_for(d)
            part = product(rows)
            halves[a, 0, rows, :] = part[:, :HALF].astype(BF16)
            halves[a, 1, rows, :] = part[:, HALF:].astype(BF16)
            remote(
                halves.at[a, 1 - core, rows], sibrecv.at[a, rows], s1send.at[a, d], s1recv.at[a, d], sibling, rep
            ).start()

    def grad_to_layer(a):
        for d in (0, 1):
            rows = rows_for(d)
            wait_for(sibrecv.at[a, rows], s1recv.at[a, d])
            both = halves[a, core, rows, :].astype(F32) + sibrecv[a, rows, :].astype(F32)
            owned = pl.ds(pl.multiple_of(lax.rem(xlo + d, 2) * REPS, REPS), REPS)
            pieces[a, owned] = both.astype(BF16).reshape(REPS, PIECE, HALF)
            for xl, to in layer[:7] if d == 0 else layer[7:]:
                remote(
                    pieces.at[a, xl * REPS + to], piecerecv.at[a, mine], p1send.at[a], p1recv.at[a],
                    row_at(xl, z, core), to,
                ).start()

    def grad_to_ring(a):
        total = pieces[a, mine].astype(F32)
        wait_for(piecerecv.at[a, pl.ds(0, CHIPS - 1)], p1recv.at[a])
        for xl, other in layer:
            total += piecerecv[a, xl * REPS + other].astype(F32)
        ringrecv[a, z] = total.astype(BF16)
        for d in (4, 3, 5, 2, 6, 1, 7):
            place = ringrecv.at[a, z]
            to = row_at(xlo, around(z + d), core)
            remote(place, place, r1send.at[a], r1recv.at[a], to, rep).start()

    def grad_from_ring(a):
        wait_for(ringrecv.at[a, pl.ds(0, NZ - 1)], r1recv.at[a])
        total = ringrecv[a, 0].astype(F32)
        for zz in range(1, NZ):
            total += ringrecv[a, zz].astype(F32)
        full[a, core, mine] = total.astype(BF16)
        piece = full.at[a, core, mine]
        for xl, to in layer:
            remote(piece, piece, q1send.at[a], q1recv.at[a], row_at(xl, z, core), to).start()

    def grad_share(a):
        wait_for(full.at[a, core, pl.ds(0, CHIPS - 1)], q1recv.at[a])
        half = full.at[a, core]
        remote(half, half, s2send.at[a], s2recv.at[a], sibling, rep).start()

    def grad_end(a):
        wait_for(full.at[a, 1 - core], s2recv.at[a])

    def grad_drain(a):
        for d in (0, 1):
            wait_for(sibrecv.at[a, rows_for(d)], s1send.at[a, d])
        wait_for(piecerecv.at[a, pl.ds(0, CHIPS - 1)], p1send.at[a])
        wait_for(ringrecv.at[a, pl.ds(0, NZ - 1)], r1send.at[a])
        wait_for(full.at[a, core, pl.ds(0, CHIPS - 1)], q1send.at[a])
        wait_for(full.at[a, core], s2send.at[a])

    def lay_out_strip():
        inputs[2].wait()

        def merge(k, _):
            for b in range(SLOTS):
                where = coords_ref[0, k, 0, b] * SLOTS + coords_ref[0, k, 1, b]
                codes[k * SLOTS + b] = jnp.where(b < counts_ref[0, k], where, 255)
            for b in range(SLOTS):
                total = a_ref[0, k, b].astype(F32)
                for other in range(b):
                    same = codes[k * SLOTS + other] == codes[k * SLOTS + b]
                    total += a_ref[0, k, other].astype(F32) * jnp.where(same, 1.0, 0.0)
                merged[k, b] = total.astype(BF16)
            merged[k, SLOTS] = jnp.zeros((BLK, BLK), BF16)
            return None

        lax.fori_loop(0, TILES, merge, None)

        def place(zz, _):
            parity, from_y = maker(zz)
            for xl in (0, 1):
                q = NY * xl + from_y
                for cc in (0, 1):
                    k = 2 * parity + cc
                    for i in range(SLOTS):
                        slot = SLOTS
                        for b in range(SLOTS):
                            slot = jnp.where(codes[k * SLOTS + b] == i * SLOTS + q, b, slot)
                        dense[xl, zz, i * BLK:(i + 1) * BLK, cc * BLK:(cc + 1) * BLK] = merged[k, slot]
            return None

        lax.fori_loop(0, NZ, place, None)

    swap_own(0)
    slab_start()
    slab_own()
    lay_out_strip()
    for copy in inputs[3:]:
        copy.wait()
    selfpre[...] = jnp.dot(x_ref[...], ws_ref[...], preferred_element_type=F32) + bias_ref[...]
    gather(0, {})
    half_columns = [slice(h * HALF, (h + 1) * HALF) for h in (0, 1)]
    for h, columns in enumerate(half_columns):
        halfsend[h] = acc[:, columns].astype(BF16).reshape(REPS, BLK, HALF)
        for to in others:
            remote(halfsend.at[h, to], halfrecv.at[h, rep], rssend.at[0], halfsem.at[h], row, to).start()
    pre_halves = []
    for h, columns in enumerate(half_columns):
        total = acc[pl.ds(pl.multiple_of(rep * BLK, BLK), BLK), columns] + selfpre[:, columns]
        wait_for(halfrecv.at[h, pl.ds(0, REPS - 1)], halfsem.at[h])
        for other in others:
            total += halfrecv[h, other].astype(F32)
        sigma = jax.nn.sigmoid(total)
        slope = og_ref[:, columns].astype(F32) * sigma * (1.0 + total * (1.0 - sigma))
        own[1, h] = slope.astype(BF16)
        swap_own(1, (h,))
        act_ref[:, columns] = (total * sigma).astype(BF16)
    pre_grad = jnp.concatenate([own[1, 0], own[1, 1]], axis=1)
    grad_start(0, lambda rows: jnp.dot(slab[rep, rows, :], pre_grad, preferred_element_type=F32))
    fg_self = lax.dot_general(pre_grad, ws_ref[...], (((1,), (1,)), ((), ())), preferred_element_type=F32)
    grad_to_layer(0)
    slab_other()

    gather(1, {
        "stepped": lambda: grad_to_ring(0),
        "gathered": lambda: grad_from_ring(0),
    })
    round_partial(1)
    slab_end()

    def slab_product(rows):
        total = jnp.zeros((FIN // 2, FO), F32)
        for pair in range(REPS // 2):
            left = jnp.concatenate([slab[2 * pair, rows, :], slab[2 * pair + 1, rows, :]], axis=1)
            right = psend[1, 2 * pair:2 * pair + 2].reshape(2 * BLK, FO)
            total += jnp.dot(left, right, preferred_element_type=F32)
        return total

    grad_start(1, slab_product)
    grad_to_layer(1)
    total = jnp.zeros((8, FO), F32)
    ones = jnp.ones((8, 2 * BLK), BF16)
    for xl in (0, 1):
        for zz in range(NZ):
            both = jnp.concatenate([units[1, 0, xl, zz], units[1, 1, xl, zz]], axis=1)
            total += jnp.dot(ones, both, preferred_element_type=F32)
    bown[...] = total
    for to in others:
        remote(bown, brecv.at[rep], bsend, bread, row, to).start()
    grad_to_ring(1)
    scatter(1)
    grad_share(0)
    grad_from_ring(1)
    hidden = collect(1).astype(BF16)
    fg_ref[...] = (
        fg_self + lax.dot_general(hidden, wn_ref[...], (((1,), (1,)), ((), ())), preferred_element_type=F32)
    ).astype(BF16)
    wait_for(brecv.at[pl.ds(0, REPS - 1)], bread)
    brecv[rep] = bown[...]
    total = brecv[0, 0:1, :]
    for q in range(1, REPS):
        total += brecv[q, 0:1, :]
    bg_ref[...] = total
    grad_end(0)
    for which in (0, 1):
        for k in (0, 1):
            for h in (0, 1):
                @pl.when(elsewhere(goal(k, h), goal_rep))
                def _():
                    wait_for(own.at[which, h], asend.at[which, 2 * k + h])

        wait_for(units.at[which, 0, 0, pl.ds(0, 2)], xsend.at[which])
        wait_for(units.at[which, 0, 0, pl.ds(0, 6)], zsend.at[which])
        wait_for(units.at[which, 0, 0, pl.ds(0, 6)], dsend.at[which])
        wait_for(units.at[which, 0], csend.at[which])
        wait_for(psend.at[which, pl.ds(0, REPS - 1)], rssend.at[which])
    wait_for(brecv.at[pl.ds(0, REPS - 1)], bsend)
    wait_for(slab.at[pl.ds(0, REPS - 1)], slabsend)
    grad_drain(0)
    grad_share(1)
    grad_end(1)
    grad_drain(1)


def finish(act_in, fg_in, full, bias_in, act_ref, fg_ref, sg_ref, ng_ref, bg_ref):
    scale = NODES ** -0.5
    rows = FIN // PARTS
    for a, out_ref in enumerate((sg_ref, ng_ref)):
        for h in (0, 1):
            out_ref[:, h * HALF:(h + 1) * HALF] = full[a, h].reshape(rows, HALF).astype(F32) * scale
    act_ref[...] = act_in[...]
    fg_ref[...] = fg_in[...]
    bg_ref[...] = bias_in[...] * scale


def shards(node_features, self_weight, neigh_weight, bias, block_values, block_coords, block_counts, out_grad):
    vmem = pl.BlockSpec(memory_space=pltpu.VMEM)
    smem = pl.BlockSpec(memory_space=pltpu.SMEM)
    hbm = pl.BlockSpec(memory_space=pltpu.HBM)
    dma = pltpu.SemaphoreType.DMA
    outs = pl.pallas_call(
        kernel,
        out_shape=(
            jax.ShapeDtypeStruct((BLK, FO), BF16),
            jax.ShapeDtypeStruct((BLK, FIN), BF16),
            jax.ShapeDtypeStruct((2, 2, CHIPS, PIECE, HALF), BF16),
            jax.ShapeDtypeStruct((1, FO), F32),
        ),
        in_specs=[hbm, hbm, hbm, hbm, hbm, smem, smem, hbm],
        out_specs=(vmem,) * 4,
        scratch_shapes=[
            pltpu.VMEM((BLK, FIN), BF16),
            pltpu.VMEM((FIN, FO), BF16),
            pltpu.VMEM((FIN, FO), BF16),
            pltpu.VMEM((1, FO), F32),
            pltpu.VMEM((1, TILES, SLOTS, BLK, BLK), BF16),
            pltpu.VMEM((BLK, FO), BF16),
            dma((6,)),
            pltpu.SMEM((TILES * SLOTS,), jnp.int32),
            pltpu.VMEM((TILES, SLOTS + 1, BLK, BLK), BF16),
            pltpu.VMEM((2, NZ, SLOTS * BLK, 2 * BLK), BF16),
            pltpu.VMEM((2, 2, 2, NZ, 2 * BLK, HALF), BF16),
            pltpu.VMEM((2, 2, BLK, HALF), BF16),
            pltpu.VMEM((SLOTS * BLK, FO), F32),
            pltpu.VMEM((2, REPS, BLK, FO), BF16),
            pltpu.VMEM((2, REPS, BLK, FO), BF16),
            pltpu.VMEM((BLK, FO), F32),
            pltpu.VMEM((2, 2, FIN, HALF), BF16),
            pltpu.VMEM((2, FIN, HALF), BF16),
            pltpu.VMEM((2, CHIPS, PIECE, HALF), BF16),
            pltpu.VMEM((2, CHIPS, PIECE, HALF), BF16),
            pltpu.VMEM((2, NZ, PIECE, HALF), BF16),
            pltpu.VMEM((8, FO), F32),
            pltpu.VMEM((REPS, 8, FO), F32),
            pltpu.VMEM((REPS, FIN, BLK), BF16),
            pltpu.VMEM((2, REPS, BLK, HALF), BF16),
            pltpu.VMEM((2, REPS, BLK, HALF), BF16),
            dma((2,)),
            dma((2, 4)), dma((2, 2 * NZ)), dma((2, 2 * NZ)), dma((2, 4)),
            dma((2,)), dma((2,)), dma((2,)), dma((2,)), dma((2,)), dma((2,)),
            dma((2, 2)), dma((2, 2)), dma((2,)), dma((2,)), dma((2,)), dma((2,)),
            dma((2,)), dma((2,)), dma((2,)), dma((2,)),
            dma, dma, dma, dma((3,)),
        ],
        compiler_params=pltpu.CompilerParams(
            collective_id=0, has_side_effects=True, vmem_limit_bytes=56 * 1024 * 1024
        ),
        cost_estimate=pl.CostEstimate(flops=5 * 10 ** 9, bytes_accessed=6 * 10 ** 6, transcendentals=BLK * FO),
        name="sage_layer",
    )(
        node_features, self_weight, neigh_weight, bias.reshape(1, FO), block_values, block_coords.swapaxes(2, 3), block_counts,
        out_grad,
    )
    act, fg, sg, ng, bg = pl.pallas_call(
        finish,
        out_shape=(
            jax.ShapeDtypeStruct((BLK, FO), BF16),
            jax.ShapeDtypeStruct((BLK, FIN), BF16),
            jax.ShapeDtypeStruct((FIN, FO), F32),
            jax.ShapeDtypeStruct((FIN, FO), F32),
            jax.ShapeDtypeStruct((1, FO), F32),
        ),
        grid=(PARTS,),
        in_specs=[
            pl.BlockSpec((BLK // PARTS, FO), lambda i: (i, 0)),
            pl.BlockSpec((BLK // PARTS, FIN), lambda i: (i, 0)),
            pl.BlockSpec((2, 2, CHIPS // PARTS, PIECE, HALF), lambda i: (0, 0, i, 0, 0)),
            pl.BlockSpec((1, FO), lambda i: (0, 0)),
        ],
        out_specs=(
            pl.BlockSpec((BLK // PARTS, FO), lambda i: (i, 0)),
            pl.BlockSpec((BLK // PARTS, FIN), lambda i: (i, 0)),
            pl.BlockSpec((FIN // PARTS, FO), lambda i: (i, 0)),
            pl.BlockSpec((FIN // PARTS, FO), lambda i: (i, 0)),
            pl.BlockSpec((1, FO), lambda i: (0, 0)),
        ),
        compiler_params=pltpu.CompilerParams(vmem_limit_bytes=56 * 1024 * 1024),
        name="finish",
    )(*outs)
    return act, fg, sg, ng, bg.reshape(FO)


def solution(mesh):
    nodes = P(("row", "rep"), None)
    placed = (
        nodes, P(), P(), P(), P("row", "rep", None, None, None), P("row", "rep", None, None), P("row", "rep"), nodes,
    )
    return jax.shard_map(
        shards, mesh=mesh, in_specs=placed, out_specs=(nodes, nodes, P(), P(), P()), check_vma=False
    )
```
